128 devices in a mesh: sec: 4 (over y), dev: 32 (over z, x, core).
Axes of the slice: x: 4, y: 4, z: 4, core: 2. Of those that a mesh axis runs over, the one named last changes fastest.
Arguments:
- moe_input: bfloat16 [512, 7168], P(('sec', 'dev')), may hold values from -6 to 6
- expert_ids: int32 [512, 8], P(('sec', 'dev')), may hold values from 0 to 31, all different within a row; in each aligned block of 4 rows (0 to 3, 4 to 7, ...) at most 2 rows name the same one
- gate_weights: float32 [512, 8], P(('sec', 'dev')), may hold values from 0.1 to 0.6
- capacity: int32 [32], replicated, may hold values from 64 to 256
- gate_proj: bfloat16 [32, 7168, 2048], P('dev', None, 'sec'), may hold values from -0.0625 to 0.0625
- up_proj: bfloat16 [32, 7168, 2048], P('dev', None, 'sec'), may hold values from -0.0625 to 0.0625
- down_proj: bfloat16 [32, 2048, 7168], P('dev', 'sec'), may hold values from -0.125 to 0.125
- queries: bfloat16 [128, 128, 576], P(('sec', 'dev')), may hold values from -5 to 5
- latent_cache: bfloat16 [128, 2048, 576], P(('sec', 'dev')), may hold values from -5 to 5
- lengths: int32 [128], P(('sec', 'dev')), may hold values from 256 to 2048
Outputs:
- moe_output: bfloat16 [512, 7168], P(('sec', 'dev'))
- attn_output: bfloat16 [128, 128, 512], P(('sec', 'dev'))
The draws below stay inside these ranges and needn't reach their ends.
Inputs may be any that keep to these rules, and one draw needn't show every extreme that they name: `expert_ids`: the 4 rows of one device name one expert at most 2 times; some device's rows name some expert exactly 2 times.
All inputs are finite; a program needn't handle non-finite values.
Results may differ from the reference program's by a relative error of at most 0.009.
Values may be sent and summed in bfloat16 or wider, within the bound.
A program may use at most 128 MiB of HBM per device.

```python
import math
import jax
import jax.numpy as jnp
import numpy as np
from jax import lax

D = 7168
EXPERT_FF = 2048
HEADS = 128
LATENT = 512
ROPE = 64
TOP = 8
EXPERTS = 32
TOK_DEV = 4
CACHE = 2048
TOKENS = 512
SEQS = 128
HID_DEV = 512
SLOT = 2
N_SEC = 4
N_DEV = 32


def draw_queries(key, part):
    key = jax.random.fold_in(key, 11)
    values = jnp.clip(jax.random.normal(key, (SEQS, HEADS, LATENT + ROPE), jnp.float32), -5.0, 5.0)
    return values.astype(jnp.bfloat16)


def draw_latent_cache(key, part):
    key = jax.random.fold_in(key, 13)
    values = jnp.clip(jax.random.normal(key, (SEQS, CACHE, LATENT + ROPE), jnp.float32), -5.0, 5.0)
    return values.astype(jnp.bfloat16)


def draw_lengths(key, part):
    key = jax.random.fold_in(key, 5)
    first, second = jax.random.split(key)
    values = jax.random.randint(first, (SEQS,), CACHE // 8, CACHE + 1, dtype=jnp.int32)
    order = jax.random.permutation(second, SEQS)
    return values.at[order[0]].set(CACHE).at[order[1]].set(CACHE // 8)


def draw_capacity(key, part):
    key = jax.random.fold_in(key, 7)
    first, second = jax.random.split(key)
    lowest = TOKENS * TOP // EXPERTS // 2
    highest = 2 * TOKENS * TOP // EXPERTS
    values = jax.random.randint(first, (EXPERTS,), lowest, highest + 1, dtype=jnp.int32)
    order = jax.random.permutation(second, EXPERTS)
    return values.at[order[0]].set(highest).at[order[1]].set(lowest)


def levels(rng, shape, cuts, low, high):
    def one(dim, shards_of):
        steps = jax.random.uniform(jax.random.fold_in(jax.random.fold_in(rng, 6), dim), (shards_of,), jnp.float32, low / len(cuts), high / len(cuts))
        return jnp.repeat(jnp.exp(steps), shape[dim] // shards_of).reshape((-1,) + (1,) * (len(shape) - dim - 1))

    loudness = one(*cuts[0])
    for cut in cuts[1:]:
        loudness = loudness * one(*cut)
    return loudness


def routed_block(own_key, own, number, rows, count, top, reach, slope):
    order = jax.random.permutation(own_key, count)
    crowded, common = portions_of(count, rows * top, reach, slope, True), portions_of(count, rows * top, reach, slope, False)
    places = jnp.arange(count)

    def named(sizes, rotation):
        used = int((sizes > 0).sum())
        fixed = max(1, used // 4)
        passed = fixed + (places - fixed + rotation * (used - fixed)) % max(1, count - fixed)
        return jnp.zeros((count,), jnp.int32).at[order[jnp.where(places < fixed, places, passed)]].set(jnp.asarray(sizes, jnp.int32))

    sizes = jnp.where(number % 4 == 0, named(crowded, number // 4), named(common, number - number // 4 - 1))
    mixed = jax.random.permutation(jax.random.fold_in(own, 3), count)
    donor, taker = mixed[0:count // 2 * 2:2], mixed[1:count // 2 * 2:2]
    margin = jnp.minimum(sizes[donor] - 1, reach - sizes[taker]) // 2
    margin = jnp.where((donor == order[0]) | (taker == order[0]) | (sizes[taker] == 0), 0, jnp.maximum(margin, 0))
    passed = jax.random.randint(jax.random.fold_in(own, 4), (count // 2,), 0, 1 << 20) % (margin + 1)
    sizes = sizes.at[donor].add(-passed).at[taker].add(passed)
    labels = jnp.searchsorted(jnp.cumsum(sizes), jnp.arange(rows * top), side="right").astype(jnp.int32)
    table = labels.reshape(top, rows).T
    table = table[jax.random.permutation(jax.random.fold_in(own, 1), rows)]
    rotation = jax.random.randint(jax.random.fold_in(own, 2), (rows, 1), 0, top)
    return jnp.take_along_axis(table, (jnp.arange(top)[None, :] + rotation) % top, axis=1)


def portions_of(count, total, most, skew, full):
    weights = [(1 << 20) // math.isqrt(grade ** skew) + 1 for grade in range(1, count + 1)]
    largest = most if full else min(most, max(-(-total // count), total * weights[0] // sum(weights)))
    least = 1 if total - largest >= count - 1 else 0
    given, spare = [largest] + [least] * (count - 1), total - largest - least * (count - 1)
    while spare > 0:
        movable = [i for i in range(1, count) if given[i] < largest] or [i for i in range(1, count) if given[i] < most]
        mass, budget = sum([weights[i] for i in movable]), spare
        for i in movable:
            extra = min(most - given[i], max(1, budget * weights[i] // mass), spare)
            given[i] = given[i] + extra
            spare = spare - extra
    return np.array(given)


def centred(own_key, extent, deviation, most, cuts=(), kind=jnp.bfloat16):
    loudness = levels(own_key, extent, cuts, -0.22, 0.18) if cuts else 1.0
    drawn = jax.random.normal(own_key, extent, jnp.float32) * deviation * loudness
    return jnp.minimum(jnp.maximum(drawn, -most), most).astype(kind)


def setup_inputs(seed: int = 0) -> dict:
    key_of = jax.random.split(jax.random.key(seed), 11)
    moe_input = centred(key_of[0], (TOKENS, D), 1.0, 6.0, ((0, 128),))
    expert_ids_keys = jax.random.split(jax.random.fold_in(key_of[1], 1), TOKENS // TOK_DEV)
    expert_ids_turns = jax.random.permutation(jax.random.fold_in(key_of[1], 3), TOKENS // TOK_DEV)
    expert_ids = jax.vmap(lambda own, number: routed_block(jax.random.fold_in(key_of[1], 2), own, number, TOK_DEV, EXPERTS, TOP, SLOT, 2))(expert_ids_keys, expert_ids_turns).reshape((TOKENS, TOP))
    gate_weights = jnp.clip(0.1 + 0.5 * jax.random.uniform(key_of[2], (TOKENS, TOP), jnp.float32) ** levels(key_of[2], (TOKENS, TOP), ((0, 128),), -0.2, 0.2), 0.1, 0.6)
    capacity = draw_capacity(jax.random.fold_in(key_of[10], 71), 0)
    gate_proj = centred(key_of[4], (EXPERTS, D, EXPERT_FF), D ** -0.5, 0.0625, ((0, 32), (2, 4)))
    up_proj = centred(key_of[5], (EXPERTS, D, EXPERT_FF), D ** -0.5, 0.0625, ((0, 32), (2, 4)))
    down_proj = centred(key_of[6], (EXPERTS, EXPERT_FF, D), EXPERT_FF ** -0.5, 0.125, ((0, 32), (1, 4)))
    queries = draw_queries(jax.random.fold_in(key_of[10], 71), 0)
    latent_cache = draw_latent_cache(jax.random.fold_in(key_of[10], 71), 0)
    lengths = draw_lengths(jax.random.fold_in(key_of[10], 71), 0)
    return {"moe_input": moe_input, "expert_ids": expert_ids, "gate_weights": gate_weights, "capacity": capacity, "gate_proj": gate_proj, "up_proj": up_proj, "down_proj": down_proj, "queries": queries, "latent_cache": latent_cache, "lengths": lengths}


softmax_scale = 192.0 ** -0.5


def attend(queries, latent_cache, lengths):
    def one_request(packed):
        query_rows, cache_rows, length_one = packed
        scores = jnp.dot(query_rows, cache_rows.T, preferred_element_type=jnp.float32) * softmax_scale
        position = jnp.arange(CACHE, dtype=jnp.int32)
        scores = jnp.where(position[None, :] < length_one, scores, -jnp.inf)
        largest = jnp.max(scores, axis=1, keepdims=True)
        expo = jnp.exp(scores - largest)
        probs = (expo / jnp.sum(expo, axis=1, keepdims=True)).astype(jnp.bfloat16)
        return jnp.dot(probs, cache_rows[:, :LATENT], preferred_element_type=jnp.float32).astype(jnp.bfloat16)

    return lax.map(one_request, (queries, latent_cache, lengths))


def reference(moe_input, expert_ids, gate_weights, capacity, gate_proj, up_proj, down_proj, queries, latent_cache, lengths):
    devices = N_SEC * N_DEV
    one_hot = (expert_ids[:, :, None] == jnp.arange(EXPERTS, dtype=jnp.int32)[None, None, :]).astype(jnp.int32)
    row_counts = jnp.sum(one_hot, axis=1)
    before_all = jnp.cumsum(row_counts, axis=0) - row_counts
    arrival = jnp.sum(one_hot * before_all[:, None, :], axis=2)
    kept = jnp.where(arrival < capacity[expert_ids], gate_weights, 0.0).astype(jnp.float32)
    grouped = row_counts.reshape(devices, TOK_DEV, EXPERTS)
    before_local = (jnp.cumsum(grouped, axis=1) - grouped).reshape(TOKENS, EXPERTS)
    local_rank = jnp.sum(one_hot * before_local[:, None, :], axis=2)
    source = jnp.arange(TOKENS, dtype=jnp.int32) // TOK_DEV
    slot_flat = ((expert_ids * devices + source[:, None]) * SLOT + local_rank).reshape(-1).astype(jnp.int32)
    row_index = jnp.broadcast_to(jnp.arange(TOKENS, dtype=jnp.int32)[:, None], (TOKENS, TOP)).reshape(-1)
    table = jnp.zeros((EXPERTS * devices * SLOT,), jnp.int32).at[slot_flat].set(row_index).reshape(EXPERTS, devices * SLOT)
    weight_table = jnp.zeros((EXPERTS * devices * SLOT,), jnp.float32).at[slot_flat].set(kept.reshape(-1)).reshape(EXPERTS, devices * SLOT)

    def expert_step(mixed, expert):
        chosen_rows = table[expert]
        chosen = moe_input[chosen_rows]
        gate_val = jnp.dot(chosen, gate_proj[expert], preferred_element_type=jnp.float32)
        up_val = jnp.dot(chosen, up_proj[expert], preferred_element_type=jnp.float32)
        hidden = (jax.nn.silu(gate_val) * up_val).astype(jnp.bfloat16)
        total = jnp.zeros((devices * SLOT, D), jnp.float32)
        for block in range(N_SEC):
            piece = jnp.dot(hidden[:, block * HID_DEV:(block + 1) * HID_DEV], down_proj[expert, block * HID_DEV:(block + 1) * HID_DEV], preferred_element_type=jnp.float32).astype(jnp.bfloat16)
            piece = lax.optimization_barrier(piece)
            total = total + piece.astype(jnp.float32)
        expert_rows = total.astype(jnp.bfloat16).astype(jnp.float32)
        mixed = mixed.at[chosen_rows].add(weight_table[expert][:, None] * expert_rows)
        return mixed, None

    mixed, unused = lax.scan(expert_step, jnp.zeros((TOKENS, D), jnp.float32), jnp.arange(EXPERTS, dtype=jnp.int32))
    return mixed.astype(jnp.bfloat16), attend(queries, latent_cache, lengths)
```

```python
import functools

import jax
import jax.numpy as jnp
from jax import lax
from jax.experimental import pallas as pl
from jax.experimental.pallas import tpu as pltpu
from jax.sharding import PartitionSpec as P

MESH = pl.DeviceIdType.MESH
BF16 = jnp.bfloat16
F32 = jnp.float32
LATENT = 512
D = 7168
HID = 512
HEADS = 128
CACHE = 2048
EXPERTS = 32
TOP = 8
LANE = 128
PART = 19 * LANE
FOLD = 5 * LANE
SUBS = ((0, 10), (10, 9))
NSUB = len(SUBS)
ORDERS = ("xyz", "yzx", "zxy")
SCALE = 192.0 ** (-0.5)


def span(p, s):
    off, count = SUBS[s]
    skip = LANE if (p == 2 and s == 0) else 0
    start = p * PART + off * LANE + skip - (LANE if p == 2 else 0)
    return skip, count * LANE - skip, start


def mm(a, b):
    return jnp.dot(a, b, preferred_element_type=F32)


def nt(a, b):
    return lax.dot_general(a, b, (((1,), (1,)), ((), ())), preferred_element_type=F32)


def tn(a, b):
    return lax.dot_general(a, b, (((0,), (0,)), ((), ())), preferred_element_type=F32)


def axes_of(i, p):
    a = {ORDERS[p][2]: (i >> 6) & 3, ORDERS[p][1]: (i >> 4) & 3, ORDERS[p][0]: (i >> 2) & 3}
    return a["x"], a["y"], a["z"], (i >> 8) & 1, i & 3


def token_of(i, p):
    x, y, z, c, r = axes_of(i, p)
    return y * 128 + z * 32 + x * 8 + c * 4 + r


def place_of(i, p):
    x, y, z, _, _ = axes_of(i, p)
    return y * 16 + x * 4 + z


def kernel(
    lengths_ref, capacity_ref, x_ref, ids_ref, gw_ref, q_hbm, kv_hbm, gate_hbm, up_hbm, down_hbm,
    out_ref, attn_ref,
    q, kv, gate, up, down, scores, probs,
    fold, s1, xb, sel, kept_col, packed, acc_g, acc_u, ht,
    cs, cr, rv, us, rw, vq, d3, r3,
    lsem, s1_sem, g2_sem, g3_sem, cx_sem, r0_sem, r1_sem, r2_sem, r3_sem,
):
    y = lax.axis_index("sec")
    dev = lax.axis_index("dev")
    z, x, c = dev // 8, (dev // 2) % 4, dev % 2
    at = {"x": x, "y": y, "z": z}

    def peer(axis, step):
        to = dict(at)
        to[axis] = (at[axis] + step + 4) % 4
        return (to["y"], to["z"] * 8 + to["x"] * 2 + c)

    sibling = (y, z * 8 + x * 2 + (1 - c))
    barrier = pltpu.get_barrier_semaphore()
    for axis in "xyz":
        for step in (1, 2, 3):
            pl.semaphore_signal(barrier, inc=1, device_id=peer(axis, step), device_id_type=MESH)
    pl.semaphore_signal(barrier, inc=1, device_id=sibling, device_id_type=MESH)

    local = {}
    for n, (src, dst) in enumerate(
        ((q_hbm.at[0], q), (kv_hbm.at[0], kv), (gate_hbm.at[0], gate), (up_hbm.at[0], up), (down_hbm.at[0], down))
    ):
        local[n] = pltpu.make_async_copy(src, dst, lsem.at[n])
        local[n].start()

    sent = {}

    def send(key, sems, index, src, dst, to):
        copy = pltpu.make_async_remote_copy(
            src_ref=src, dst_ref=dst,
            send_sem=sems.at[(0,) + index], recv_sem=sems.at[(1,) + index],
            device_id=to, device_id_type=MESH,
        )
        copy.start()
        sent[key] = copy

    def got(key):
        sent[key].wait_recv()

    lane = lax.broadcasted_iota(jnp.int32, (4, LANE), 1)
    info = jnp.zeros((4, LANE), F32)
    ids = ids_ref[...]
    gw = gw_ref[...]
    high = gw.astype(BF16).astype(F32)
    mid = (gw - high).astype(BF16).astype(F32)
    low = gw - high - mid
    for k in range(TOP):
        for n, piece in enumerate((high, mid, low)):
            info = info + jnp.where(lane == ids[:, k:k + 1] + n * EXPERTS, piece[:, k:k + 1], 0.0)
    fold[...] = jnp.zeros_like(fold)
    for p in range(3):
        for f in range(4):
            first, width = f * FOLD, min(FOLD, PART - f * FOLD)
            lead = LANE if (p == 2 and f == 0) else 0
            start = p * PART + first + lead - (LANE if p == 2 else 0)
            fold[p, 4 * f:4 * f + 4, lead:width] = x_ref[:, start:start + width - lead].astype(F32)
    fold[2, 0:4, 0:LANE] = info
    for p in range(3):
        s1[p, at[ORDERS[p][0]]] = fold[p].astype(BF16)
    pl.semaphore_wait(barrier, 10)
    for step in (1, 2, 3):
        for p in range(3):
            axis = ORDERS[p][0]
            mine = s1.at[p, at[axis]]
            send(("s1", p, step), s1_sem, (p, step - 1), mine, mine, peer(axis, step))

    def attend_scores():
        local[0].wait()
        local[1].wait()
        position = lax.broadcasted_iota(jnp.int32, (1, 512), 1)
        length = lengths_ref[0]
        for n in range(CACHE // 512):
            rows = kv[n * 512:(n + 1) * 512, :]
            score = nt(q[:, :LATENT], rows[:, :LATENT]) + nt(q[:, LATENT:], rows[:, LATENT:])
            scores[:, n * 512:(n + 1) * 512] = jnp.where(position + n * 512 < length, score * SCALE, -jnp.inf)

    def attend_probs():
        score = scores[...]
        expo = jnp.exp(score - jnp.max(score, axis=1, keepdims=True))
        probs[...] = (expo / jnp.sum(expo, axis=1, keepdims=True)).astype(BF16)

    def attend_values():
        attn_ref[0] = mm(probs[...], kv[:, :LATENT]).astype(BF16)

    i0 = lax.broadcasted_iota(jnp.int32, (64, 64), 0)
    i1 = lax.broadcasted_iota(jnp.int32, (64, 64), 1)
    turn = jnp.where(((i0 >> 4) == ((i1 >> 2) & 3)) & (((i0 >> 2) & 3) == (i1 >> 4)) & ((i0 & 3) == (i1 & 3)), 1.0, 0.0).astype(BF16)

    def block(p, n, size):
        return pl.ds(pl.multiple_of(n * size, size), size)

    def g2a(p):
        a1, a2, a3 = ORDERS[p]
        for step in (1, 2, 3):
            got(("s1", p, step))
        rows = mm(turn, s1[p].reshape(64, FOLD)).astype(BF16)
        own = block(p, at[a3] * 4 + at[a2], 16)
        for f in range(4):
            for t in range(5):
                tile = 5 * f + t
                for s, (off, count) in enumerate(SUBS):
                    if off <= tile < off + count:
                        xb[s][p, c, own, (tile - off) * LANE:(tile - off + 1) * LANE] = rows[16 * f:16 * f + 16, t * LANE:(t + 1) * LANE]
        for s in range(NSUB):
            ref = xb[s].at[p, c, own]
            send(("g2", p, s, 0), g2_sem, (p, s, 0), ref, ref, peer(a2, 1))
            send(("g2", p, s, 1), g2_sem, (p, s, 1), ref, ref, peer(a2, -1))

    def g2b(p, s):
        _, a2, a3 = ORDERS[p]
        way = 0 if (p + s) % 2 == 0 else 1
        got(("g2", p, s, way))
        off = -1 if way == 0 else 1
        ref = xb[s].at[p, c, block(p, at[a3] * 4 + (at[a2] + off + 4) % 4, 16)]
        send(("g2", p, s, 2), g2_sem, (p, s, 2), ref, ref, peer(a2, -off))

    def g3a(p, s):
        _, a2, a3 = ORDERS[p]
        way = 0 if (p + s) % 2 == 0 else 1
        got(("g2", p, s, 1 - way))
        got(("g2", p, s, 2))
        ref = xb[s].at[p, c, block(p, at[a3], 64)]
        send(("g3", p, s, 0), g3_sem, (p, s, 0), ref, ref, peer(a3, 1))
        send(("g3", p, s, 1), g3_sem, (p, s, 1), ref, ref, peer(a3, -1))
        send(("cx", p, s, 0), cx_sem, (p, s, 0), ref, ref, sibling)

    def g3b(p, s):
        a3 = ORDERS[p][2]
        for way, off in ((0, -1), (1, 1)):
            got(("g3", p, s, way))
            whole = (at[a3] + off + 4) % 4
            ref = xb[s].at[p, c, block(p, whole * 2 + way, 32)]
            send(("g3", p, s, 2 + way), g3_sem, (p, s, 2 + way), ref, ref, peer(a3, -off))
            ref = xb[s].at[p, c, block(p, whole, 64)]
            send(("cx", p, s, 1 + way), cx_sem, (p, s, 1 + way), ref, ref, sibling)

    def g3c(p, s):
        a3 = ORDERS[p][2]
        got(("g3", p, s, 2))
        got(("g3", p, s, 3))
        ref = xb[s].at[p, c, block(p, (at[a3] + 2) % 4, 64)]
        send(("cx", p, s, 3), cx_sem, (p, s, 3), ref, ref, sibling)

    def cxw(p, s):
        for n in range(4):
            got(("cx", p, s, n))

    def routing():
        pick = lax.broadcasted_iota(jnp.int32, (8, LANE), 1)
        pick = jnp.where((pick < 3 * EXPERTS) & ((pick & (EXPERTS - 1)) == dev), 1.0, 0.0).astype(BF16)
        weight = jnp.concatenate([nt(pick, xb[0][2, cc, :, 0:LANE]) for cc in range(2)], axis=1)
        named = weight > 0.0
        flag = jnp.where(named, 1.0, 0.0).astype(BF16)
        rows = lax.broadcasted_iota(jnp.int32, (512, 1), 0)
        cols = lax.broadcasted_iota(jnp.int32, (1, 512), 1)
        ones = lambda cond: jnp.where(cond, 1.0, 0.0).astype(BF16)
        arrival = mm(flag, ones(token_of(rows, 2) < token_of(cols, 2)))
        rank = mm(flag, ones(((rows >> 2) == (cols >> 2)) & (rows < cols)))
        limit = capacity_ref[dev].astype(F32)
        kept = jnp.where(arrival < limit, weight, 0.0)
        code = jnp.where(named, rank + 1.0, 0.0)
        for p in range(3):
            turned = code if p == 2 else mm(code.astype(BF16), ones(token_of(rows, 2) == token_of(cols, p)))
            for cc in range(2):
                slot = lax.broadcasted_iota(jnp.int32, (128, 1), 0)
                row = lax.broadcasted_iota(jnp.int32, (1, 256), 1)
                wanted = ((slot & 1) + 1).astype(F32)
                chosen = ((slot >> 1) == place_of(row, p)) & (turned[0:1, cc * 256:(cc + 1) * 256] == wanted)
                sel[p, cc] = ones(chosen)
                if p == 2:
                    kept_col[cc * 128:(cc + 1) * 128, :] = jnp.sum(
                        jnp.where(chosen, kept[0:1, cc * 256:(cc + 1) * 256], 0.0), axis=1, keepdims=True)

    def ffn(p, s):
        skip, width, start = span(p, s)
        for cc in range(2):
            packed[cc * 128:(cc + 1) * 128, :width] = mm(sel[p, cc], xb[s][p, cc, :, skip:skip + width]).astype(BF16)
        rows = packed[:, :width]
        acc_g[...] += mm(rows, gate[start:start + width, :])
        acc_u[...] += mm(rows, up[start:start + width, :])

    def act():
        g = acc_g[...]
        hidden = (g * (1.0 / (1.0 + jnp.exp(-g))) * acc_u[...] * kept_col[...]).astype(BF16)
        for p in range(3):
            for cc in range(2):
                ht[p, cc] = tn(sel[p, cc], hidden[cc * 128:(cc + 1) * 128, :]).astype(BF16)

    def c0(p, s):
        _, width, start = span(p, s)
        cs[s][p, :, :width] = mm(ht[p, 1 - c], down[:, start:start + width]).astype(BF16)
        send(("r0", p, s), r0_sem, (p, s), cs[s].at[p, :, :width], cr[s].at[p, :, :width], sibling)

    def plus(ref, rows, width, *others):
        total = ref[rows, :width].astype(F32)
        for other in others:
            total = total + other[:, :width].astype(F32)
        return total.astype(BF16)

    def a1(p, s):
        _, width, start = span(p, s)
        mine = mm(ht[p, c], down[:, start:start + width])
        got(("r0", p, s))
        cr[s][p, :, :width] = (mine + cr[s][p, :, :width].astype(F32)).astype(BF16)
        axis = ORDERS[p][2]
        k = at[axis]
        for n, (off, half, way) in enumerate(((2, 0, 1), (2, 1, -1), (1, 1, 1), (-1, 0, -1))):
            rows = block(p, ((k + off + 4) % 4) * 2 + half, 32)
            send(("r1", p, s, n), r1_sem, (p, s, n), cr[s].at[p, rows, :width], rv[s].at[p, n, :, :width], peer(axis, way))

    def a2(p, s):
        _, width, _ = span(p, s)
        axis = ORDERS[p][2]
        k = at[axis]
        for n, (off, half, way) in enumerate(((1, 0, 1), (-1, 1, -1))):
            got(("r1", p, s, n))
            rows = block(p, ((k + off + 4) % 4) * 2 + half, 32)
            t = cr[s].at[p]
            t[rows, :width] = plus(t, rows, width, rv[s].at[p, n])
            send(("r1", p, s, 4 + n), r1_sem, (p, s, 4 + n), cr[s].at[p, rows, :width], rv[s].at[p, 4 + n, :, :width], peer(axis, way))

    def b1(p, s):
        _, width, _ = span(p, s)
        k = at[ORDERS[p][2]]
        for n in (2, 3, 4, 5):
            got(("r1", p, s, n))
        t, u, v = cr[s].at[p], us[s].at[p], rv[s].at[p]
        u[0:32, :width] = plus(t, block(p, k * 2, 32), width, v.at[3], v.at[4])
        u[32:64, :width] = plus(t, block(p, k * 2 + 1, 32), width, v.at[2], v.at[5])
        axis = ORDERS[p][1]
        k = at[axis]
        way = 1 if (p + s) % 2 == 0 else -1
        for n, (off, to) in enumerate(((2, way), (-way, -way))):
            rows = block(p, (k + off + 4) % 4, 16)
            send(("r2", p, s, n), r2_sem, (p, s, n), u.at[rows, :width], rw[s].at[p, n, :, :width], peer(axis, to))

    def b2(p, s):
        _, width, _ = span(p, s)
        axis = ORDERS[p][1]
        k = at[axis]
        way = 1 if (p + s) % 2 == 0 else -1
        got(("r2", p, s, 0))
        rows = block(p, (k + way + 4) % 4, 16)
        u = us[s].at[p]
        u[rows, :width] = plus(u, rows, width, rw[s].at[p, 0])
        send(("r2", p, s, 2), r2_sem, (p, s, 2), u.at[rows, :width], rw[s].at[p, 2, :, :width], peer(axis, way))

    def b3(p, s):
        skip, width, _ = span(p, s)
        k = at[ORDERS[p][1]]
        got(("r2", p, s, 1))
        got(("r2", p, s, 2))
        total = plus(us[s].at[p], block(p, k, 16), width, rw[s].at[p, 1], rw[s].at[p, 2])
        off = SUBS[s][0]
        for t in range(width // LANE):
            tile = off + skip // LANE + t
            f, j = tile // 5, tile % 5
            vq[p, 16 * f:16 * f + 16, j * LANE:(j + 1) * LANE] = total[:, t * LANE:(t + 1) * LANE]

    def r3a(p):
        axis = ORDERS[p][0]
        d3[p] = mm(turn, vq[p]).astype(BF16)
        for step in (1, 2, 3):
            rows = block(p, (at[axis] + step) % 4, 16)
            send(("r3", p, step), r3_sem, (p, step - 1), d3.at[p, rows], r3.at[p, step - 1], peer(axis, step))

    def r3b(p):
        axis = ORDERS[p][0]
        total = d3[p, block(p, at[axis], 16), :].astype(F32)
        for step in (1, 2, 3):
            got(("r3", p, step))
            total = total + r3[p, step - 1].astype(F32)
        fold[p] = total
        for f in range(4):
            first, width = f * FOLD, min(FOLD, PART - f * FOLD)
            lead = LANE if (p == 2 and f == 0) else 0
            start = p * PART + first + lead - (LANE if p == 2 else 0)
            out_ref[:, start:start + width - lead] = fold[p, 4 * f:4 * f + 4, lead:width].astype(BF16)

    every = lambda step, *rest: [step(p, *rest) for p in range(3)]
    acc_g[...] = jnp.zeros_like(acc_g)
    acc_u[...] = jnp.zeros_like(acc_u)
    vq[...] = jnp.zeros_like(vq)
    attend_scores()
    every(g2a)
    attend_probs()
    for s in range(NSUB):
        every(g2b, s)
    for s in range(NSUB):
        every(g3a, s)
    attend_values()
    for s in range(NSUB):
        every(g3b, s)
    every(g3c, 0)
    every(cxw, 0)
    routing()
    local[2].wait()
    local[3].wait()
    every(ffn, 0)
    for s in range(1, NSUB):
        every(g3c, s)
        every(cxw, s)
        every(ffn, s)
    act()
    local[4].wait()
    stages = (c0, a1, a2, b1, b2, b3)
    lag = (0, 0, 1, 2, 3, 4)
    for tick in range(NSUB + lag[-1]):
        for stage, late in reversed(list(zip(stages, lag))):
            s = tick - late
            if 0 <= s < NSUB and stage is not c0 and stage is not a1:
                every(stage, s)
        if tick < NSUB:
            every(c0, tick)
            every(a1, tick)
    every(r3a)
    every(r3b)
    for copy in sent.values():
        copy.wait_send()


def body(moe_input, expert_ids, gate_weights, capacity, gate_proj, up_proj, down_proj, queries, latent_cache, lengths):
    vmem = pl.BlockSpec(memory_space=pltpu.VMEM)
    smem = pl.BlockSpec(memory_space=pltpu.SMEM)
    hbm = pl.BlockSpec(memory_space=pl.ANY)
    widths = [count * LANE for _, count in SUBS]
    per_sub = lambda *lead: [pltpu.VMEM(lead + (w,), BF16) for w in widths]
    dma = lambda *shape: pltpu.SemaphoreType.DMA((2,) + shape)
    scratch = [
        pltpu.VMEM((HEADS, 576), BF16), pltpu.VMEM((CACHE, 576), BF16),
        pltpu.VMEM((D, HID), BF16), pltpu.VMEM((D, HID), BF16), pltpu.VMEM((HID, D), BF16),
        pltpu.VMEM((HEADS, CACHE), F32), pltpu.VMEM((HEADS, CACHE), BF16),
        pltpu.VMEM((3, 16, FOLD), F32), pltpu.VMEM((3, 4, 16, FOLD), BF16),
        per_sub(3, 2, 256),
        pltpu.VMEM((3, 2, 128, 256), BF16), pltpu.VMEM((256, 1), F32), pltpu.VMEM((256, max(widths)), BF16),
        pltpu.VMEM((256, HID), F32), pltpu.VMEM((256, HID), F32), pltpu.VMEM((3, 2, 256, HID), BF16),
        per_sub(3, 256), per_sub(3, 256), per_sub(3, 6, 32), per_sub(3, 64), per_sub(3, 3, 16),
        pltpu.VMEM((3, 64, FOLD), BF16), pltpu.VMEM((3, 64, FOLD), BF16), pltpu.VMEM((3, 3, 16, FOLD), BF16),
        pltpu.SemaphoreType.DMA((5,)),
        dma(3, 3), dma(3, NSUB, 3), dma(3, NSUB, 4), dma(3, NSUB, 4),
        dma(3, NSUB), dma(3, NSUB, 6), dma(3, NSUB, 3), dma(3, 3),
    ]
    return pl.pallas_call(
        kernel,
        out_shape=(jax.ShapeDtypeStruct((4, D), BF16), jax.ShapeDtypeStruct((1, HEADS, LATENT), BF16)),
        in_specs=[smem, smem, vmem, vmem, vmem, hbm, hbm, hbm, hbm, hbm],
        out_specs=(vmem, vmem),
        scratch_shapes=scratch,
        compiler_params=pltpu.CompilerParams(collective_id=0, has_side_effects=True, vmem_limit_bytes=63 << 20),
        name="fused",
    )(lengths, capacity, moe_input, expert_ids, gate_weights, queries, latent_cache, gate_proj, up_proj, down_proj)


def solution(mesh):
    placed = (
        P(("sec", "dev"), None),
        P(("sec", "dev"), None),
        P(("sec", "dev"), None),
        P(),
        P("dev", None, "sec"),
        P("dev", None, "sec"),
        P("dev", "sec", None),
        P(("sec", "dev"), None, None),
        P(("sec", "dev"), None, None),
        P(("sec", "dev")),
    )
    return jax.shard_map(
        body,
        mesh=mesh,
        in_specs=placed,
        out_specs=(P(("sec", "dev"), None), P(("sec", "dev"), None, None)),
        check_vma=False,
    )
```

```python
import functools

import jax
import jax.numpy as jnp
from jax import lax
from jax.experimental import pallas as pl
from jax.experimental.pallas import tpu as pltpu
from jax.sharding import PartitionSpec as P

MESH = pl.DeviceIdType.MESH
BF16 = jnp.bfloat16
F32 = jnp.float32
LATENT = 512
D = 7168
HID = 512
HEADS = 128
CACHE = 2048
EXPERTS = 32
TOP = 8
LANE = 128
PART = 19 * LANE
FOLD = 5 * LANE
SUBS = ((0, 10), (10, 9))
NSUB = len(SUBS)
ORDERS = ("xyz", "yzx", "zxy")
SCALE = 192.0 ** (-0.5)


def span(p, s):
    off, count = SUBS[s]
    skip = LANE if (p == 2 and s == 0) else 0
    start = p * PART + off * LANE + skip - (LANE if p == 2 else 0)
    return skip, count * LANE - skip, start


def mm(a, b):
    return jnp.dot(a, b, preferred_element_type=F32)


def nt(a, b):
    return lax.dot_general(a, b, (((1,), (1,)), ((), ())), preferred_element_type=F32)


def tn(a, b):
    return lax.dot_general(a, b, (((0,), (0,)), ((), ())), preferred_element_type=F32)


def axes_of(i, p):
    a = {ORDERS[p][2]: (i >> 6) & 3, ORDERS[p][1]: (i >> 4) & 3, ORDERS[p][0]: (i >> 2) & 3}
    return a["x"], a["y"], a["z"], (i >> 8) & 1, i & 3


def token_of(i, p):
    x, y, z, c, r = axes_of(i, p)
    return y * 128 + z * 32 + x * 8 + c * 4 + r


def place_of(i, p):
    x, y, z, _, _ = axes_of(i, p)
    return y * 16 + x * 4 + z


def kernel(
    lengths_ref, capacity_ref, x_ref, ids_ref, gw_ref, q_hbm, kv_hbm, gate_hbm, up_hbm, down_hbm,
    out_ref, attn_ref,
    q, kv, gate, up, down, scores, probs,
    fold, s1, xb, sel, kept_col, packed, acc_g, acc_u, ht,
    cs, cr, rv, us, rw, vq, d3, r3,
    lsem, s1_sem, g2_sem, g3_sem, cx_sem, r0_sem, r1_sem, r2_sem, r3_sem,
):
    y = lax.axis_index("sec")
    dev = lax.axis_index("dev")
    z, x, c = dev // 8, (dev // 2) % 4, dev % 2
    at = {"x": x, "y": y, "z": z}

    def peer(axis, step):
        to = dict(at)
        to[axis] = (at[axis] + step + 4) % 4
        return (to["y"], to["z"] * 8 + to["x"] * 2 + c)

    sibling = (y, z * 8 + x * 2 + (1 - c))
    barrier = pltpu.get_barrier_semaphore()
    for axis in "xyz":
        for step in (1, 2, 3):
            pl.semaphore_signal(barrier, inc=1, device_id=peer(axis, step), device_id_type=MESH)
    pl.semaphore_signal(barrier, inc=1, device_id=sibling, device_id_type=MESH)

    local = {}
    for n, (src, dst) in enumerate(
        ((q_hbm.at[0], q), (kv_hbm.at[0], kv), (gate_hbm.at[0], gate), (up_hbm.at[0], up), (down_hbm.at[0], down))
    ):
        local[n] = pltpu.make_async_copy(src, dst, lsem.at[n])
        local[n].start()

    sent = {}

    def send(key, sems, index, src, dst, to):
        copy = pltpu.make_async_remote_copy(
            src_ref=src, dst_ref=dst,
            send_sem=sems.at[(0,) + index], recv_sem=sems.at[(1,) + index],
            device_id=to, device_id_type=MESH,
        )
        copy.start()
        sent[key] = copy

    def got(key):
        sent[key].wait_recv()

    lane = lax.broadcasted_iota(jnp.int32, (4, LANE), 1)
    info = jnp.zeros((4, LANE), F32)
    ids = ids_ref[...]
    gw = gw_ref[...]
    high = gw.astype(BF16).astype(F32)
    mid = (gw - high).astype(BF16).astype(F32)
    low = gw - high - mid
    for k in range(TOP):
        for n, piece in enumerate((high, mid, low)):
            info = info + jnp.where(lane == ids[:, k:k + 1] + n * EXPERTS, piece[:, k:k + 1], 0.0)
    fold[...] = jnp.zeros_like(fold)
    for p in range(3):
        for f in range(4):
            first, width = f * FOLD, min(FOLD, PART - f * FOLD)
            lead = LANE if (p == 2 and f == 0) else 0
            start = p * PART + first + lead - (LANE if p == 2 else 0)
            fold[p, 4 * f:4 * f + 4, lead:width] = x_ref[:, start:start + width - lead].astype(F32)
    fold[2, 0:4, 0:LANE] = info
    for p in range(3):
        s1[p, at[ORDERS[p][0]]] = fold[p].astype(BF16)
    pl.semaphore_wait(barrier, 10)
    for step in (1, 2, 3):
        for p in range(3):
            axis = ORDERS[p][0]
            mine = s1.at[p, at[axis]]
            send(("s1", p, step), s1_sem, (p, step - 1), mine, mine, peer(axis, step))

    def attend_scores():
        local[0].wait()
        local[1].wait()
        position = lax.broadcasted_iota(jnp.int32, (1, 512), 1)
        length = lengths_ref[0]
        for n in range(CACHE // 512):
            cols = kv[:, n * 512:(n + 1) * 512]
            score = tn(q[:LATENT, :], cols[:LATENT, :]) + tn(q[LATENT:, :], cols[LATENT:, :])
            scores[:, n * 512:(n + 1) * 512] = jnp.where(position + n * 512 < length, score * SCALE, -jnp.inf)

    def attend_probs():
        score = scores[...]
        expo = jnp.exp(score - jnp.max(score, axis=1, keepdims=True))
        probs[...] = (expo / jnp.sum(expo, axis=1, keepdims=True)).astype(BF16)

    def attend_values():
        attn_ref[0] = nt(probs[...], kv[:LATENT, :]).astype(BF16)

    i0 = lax.broadcasted_iota(jnp.int32, (64, 64), 0)
    i1 = lax.broadcasted_iota(jnp.int32, (64, 64), 1)
    turn = jnp.where(((i0 >> 4) == ((i1 >> 2) & 3)) & (((i0 >> 2) & 3) == (i1 >> 4)) & ((i0 & 3) == (i1 & 3)), 1.0, 0.0).astype(BF16)

    def block(p, n, size):
        return pl.ds(pl.multiple_of(n * size, size), size)

    def g2a(p):
        a1, a2, a3 = ORDERS[p]
        for step in (1, 2, 3):
            got(("s1", p, step))
        rows = mm(turn, s1[p].reshape(64, FOLD)).astype(BF16)
        own = block(p, at[a3] * 4 + at[a2], 16)
        for f in range(4):
            for t in range(5):
                tile = 5 * f + t
                for s, (off, count) in enumerate(SUBS):
                    if off <= tile < off + count:
                        xb[s][p, c, own, (tile - off) * LANE:(tile - off + 1) * LANE] = rows[16 * f:16 * f + 16, t * LANE:(t + 1) * LANE]
        for s in range(NSUB):
            ref = xb[s].at[p, c, own]
            send(("g2", p, s, 0), g2_sem, (p, s, 0), ref, ref, peer(a2, 1))
            send(("g2", p, s, 1), g2_sem, (p, s, 1), ref, ref, peer(a2, -1))

    def g2b(p, s):
        _, a2, a3 = ORDERS[p]
        way = 0 if (p + s) % 2 == 0 else 1
        got(("g2", p, s, way))
        off = -1 if way == 0 else 1
        ref = xb[s].at[p, c, block(p, at[a3] * 4 + (at[a2] + off + 4) % 4, 16)]
        send(("g2", p, s, 2), g2_sem, (p, s, 2), ref, ref, peer(a2, -off))

    def g3a(p, s):
        _, a2, a3 = ORDERS[p]
        way = 0 if (p + s) % 2 == 0 else 1
        got(("g2", p, s, 1 - way))
        got(("g2", p, s, 2))
        ref = xb[s].at[p, c, block(p, at[a3], 64)]
        send(("g3", p, s, 0), g3_sem, (p, s, 0), ref, ref, peer(a3, 1))
        send(("g3", p, s, 1), g3_sem, (p, s, 1), ref, ref, peer(a3, -1))
        send(("cx", p, s, 0), cx_sem, (p, s, 0), ref, ref, sibling)

    def g3b(p, s):
        a3 = ORDERS[p][2]
        for way, off in ((0, -1), (1, 1)):
            got(("g3", p, s, way))
            whole = (at[a3] + off + 4) % 4
            ref = xb[s].at[p, c, block(p, whole * 2 + way, 32)]
            send(("g3", p, s, 2 + way), g3_sem, (p, s, 2 + way), ref, ref, peer(a3, -off))
            ref = xb[s].at[p, c, block(p, whole, 64)]
            send(("cx", p, s, 1 + way), cx_sem, (p, s, 1 + way), ref, ref, sibling)

    def g3c(p, s):
        a3 = ORDERS[p][2]
        got(("g3", p, s, 2))
        got(("g3", p, s, 3))
        ref = xb[s].at[p, c, block(p, (at[a3] + 2) % 4, 64)]
        send(("cx", p, s, 3), cx_sem, (p, s, 3), ref, ref, sibling)

    def cxw(p, s):
        for n in range(4):
            got(("cx", p, s, n))

    def routing():
        pick = lax.broadcasted_iota(jnp.int32, (8, LANE), 1)
        pick = jnp.where((pick < 3 * EXPERTS) & ((pick & (EXPERTS - 1)) == dev), 1.0, 0.0).astype(BF16)
        weight = jnp.concatenate([nt(pick, xb[0][2, cc, :, 0:LANE]) for cc in range(2)], axis=1)
        named = weight > 0.0
        flag = jnp.where(named, 1.0, 0.0).astype(BF16)
        rows = lax.broadcasted_iota(jnp.int32, (512, 1), 0)
        cols = lax.broadcasted_iota(jnp.int32, (1, 512), 1)
        ones = lambda cond: jnp.where(cond, 1.0, 0.0).astype(BF16)
        arrival = mm(flag, ones(token_of(rows, 2) < token_of(cols, 2)))
        rank = mm(flag, ones(((rows >> 2) == (cols >> 2)) & (rows < cols)))
        limit = capacity_ref[dev].astype(F32)
        kept = jnp.where(arrival < limit, weight, 0.0)
        code = jnp.where(named, rank + 1.0, 0.0)
        for p in range(3):
            turned = code if p == 2 else mm(code.astype(BF16), ones(token_of(rows, 2) == token_of(cols, p)))
            for cc in range(2):
                slot = lax.broadcasted_iota(jnp.int32, (128, 1), 0)
                row = lax.broadcasted_iota(jnp.int32, (1, 256), 1)
                wanted = ((slot & 1) + 1).astype(F32)
                chosen = ((slot >> 1) == place_of(row, p)) & (turned[0:1, cc * 256:(cc + 1) * 256] == wanted)
                sel[p, cc] = ones(chosen)
                if p == 2:
                    kept_col[cc * 128:(cc + 1) * 128, :] = jnp.sum(
                        jnp.where(chosen, kept[0:1, cc * 256:(cc + 1) * 256], 0.0), axis=1, keepdims=True)

    def ffn(p, s):
        skip, width, start = span(p, s)
        for cc in range(2):
            packed[cc * 128:(cc + 1) * 128, :width] = mm(sel[p, cc], xb[s][p, cc, :, skip:skip + width]).astype(BF16)
        rows = packed[:, :width]
        acc_g[...] += mm(rows, gate[start:start + width, :])
        acc_u[...] += mm(rows, up[start:start + width, :])

    def act():
        g = acc_g[...]
        hidden = (g * (1.0 / (1.0 + jnp.exp(-g))) * acc_u[...] * kept_col[...]).astype(BF16)
        for p in range(3):
            for cc in range(2):
                ht[p, cc] = tn(sel[p, cc], hidden[cc * 128:(cc + 1) * 128, :]).astype(BF16)

    def c0(p, s):
        _, width, start = span(p, s)
        cs[s][p, :, :width] = mm(ht[p, 1 - c], down[:, start:start + width]).astype(BF16)
        send(("r0", p, s), r0_sem, (p, s), cs[s].at[p, :, :width], cr[s].at[p, :, :width], sibling)

    def plus(ref, rows, width, *others):
        total = ref[rows, :width].astype(F32)
        for other in others:
            total = total + other[:, :width].astype(F32)
        return total.astype(BF16)

    def a1(p, s):
        _, width, start = span(p, s)
        mine = mm(ht[p, c], down[:, start:start + width])
        got(("r0", p, s))
        cr[s][p, :, :width] = (mine + cr[s][p, :, :width].astype(F32)).astype(BF16)
        axis = ORDERS[p][2]
        k = at[axis]
        for n, (off, half, way) in enumerate(((2, 0, 1), (2, 1, -1), (1, 1, 1), (-1, 0, -1))):
            rows = block(p, ((k + off + 4) % 4) * 2 + half, 32)
            send(("r1", p, s, n), r1_sem, (p, s, n), cr[s].at[p, rows, :width], rv[s].at[p, n, :, :width], peer(axis, way))

    def a2(p, s):
        _, width, _ = span(p, s)
        axis = ORDERS[p][2]
        k = at[axis]
        for n, (off, half, way) in enumerate(((1, 0, 1), (-1, 1, -1))):
            got(("r1", p, s, n))
            rows = block(p, ((k + off + 4) % 4) * 2 + half, 32)
            t = cr[s].at[p]
            t[rows, :width] = plus(t, rows, width, rv[s].at[p, n])
            send(("r1", p, s, 4 + n), r1_sem, (p, s, 4 + n), cr[s].at[p, rows, :width], rv[s].at[p, 4 + n, :, :width], peer(axis, way))

    def b1(p, s):
        _, width, _ = span(p, s)
        k = at[ORDERS[p][2]]
        for n in (2, 3, 4, 5):
            got(("r1", p, s, n))
        t, u, v = cr[s].at[p], us[s].at[p], rv[s].at[p]
        u[0:32, :width] = plus(t, block(p, k * 2, 32), width, v.at[3], v.at[4])
        u[32:64, :width] = plus(t, block(p, k * 2 + 1, 32), width, v.at[2], v.at[5])
        axis = ORDERS[p][1]
        k = at[axis]
        way = 1 if (p + s) % 2 == 0 else -1
        for n, (off, to) in enumerate(((2, way), (-way, -way))):
            rows = block(p, (k + off + 4) % 4, 16)
            send(("r2", p, s, n), r2_sem, (p, s, n), u.at[rows, :width], rw[s].at[p, n, :, :width], peer(axis, to))

    def b2(p, s):
        _, width, _ = span(p, s)
        axis = ORDERS[p][1]
        k = at[axis]
        way = 1 if (p + s) % 2 == 0 else -1
        got(("r2", p, s, 0))
        rows = block(p, (k + way + 4) % 4, 16)
        u = us[s].at[p]
        u[rows, :width] = plus(u, rows, width, rw[s].at[p, 0])
        send(("r2", p, s, 2), r2_sem, (p, s, 2), u.at[rows, :width], rw[s].at[p, 2, :, :width], peer(axis, way))

    def b3(p, s):
        skip, width, _ = span(p, s)
        k = at[ORDERS[p][1]]
        got(("r2", p, s, 1))
        got(("r2", p, s, 2))
        total = plus(us[s].at[p], block(p, k, 16), width, rw[s].at[p, 1], rw[s].at[p, 2])
        off = SUBS[s][0]
        for t in range(width // LANE):
            tile = off + skip // LANE + t
            f, j = tile // 5, tile % 5
            vq[p, 16 * f:16 * f + 16, j * LANE:(j + 1) * LANE] = total[:, t * LANE:(t + 1) * LANE]

    def r3a(p):
        axis = ORDERS[p][0]
        d3[p] = mm(turn, vq[p]).astype(BF16)
        for step in (1, 2, 3):
            rows = block(p, (at[axis] + step) % 4, 16)
            send(("r3", p, step), r3_sem, (p, step - 1), d3.at[p, rows], r3.at[p, step - 1], peer(axis, step))

    def r3b(p):
        axis = ORDERS[p][0]
        total = d3[p, block(p, at[axis], 16), :].astype(F32)
        for step in (1, 2, 3):
            got(("r3", p, step))
            total = total + r3[p, step - 1].astype(F32)
        fold[p] = total
        for f in range(4):
            first, width = f * FOLD, min(FOLD, PART - f * FOLD)
            lead = LANE if (p == 2 and f == 0) else 0
            start = p * PART + first + lead - (LANE if p == 2 else 0)
            out_ref[:, start:start + width - lead] = fold[p, 4 * f:4 * f + 4, lead:width].astype(BF16)

    every = lambda step, *rest: [step(p, *rest) for p in range(3)]
    acc_g[...] = jnp.zeros_like(acc_g)
    acc_u[...] = jnp.zeros_like(acc_u)
    vq[...] = jnp.zeros_like(vq)
    every(g2a)
    for s in range(NSUB):
        every(g2b, s)
    for s in range(NSUB):
        every(g3a, s)
    attend_scores()
    attend_probs()
    attend_values()
    for s in range(NSUB):
        every(g3b, s)
    every(g3c, 0)
    every(cxw, 0)
    routing()
    local[2].wait()
    local[3].wait()
    every(ffn, 0)
    for s in range(1, NSUB):
        every(g3c, s)
        every(cxw, s)
        every(ffn, s)
    act()
    local[4].wait()
    for stage in (c0, a1):
        every(stage, 0)
    for stage in (c0, a1):
        every(stage, 1)
    for stage in (a2, b1, b2, b3):
        for s in range(NSUB):
            every(stage, s)
    every(r3a)
    every(r3b)
    for copy in sent.values():
        copy.wait_send()


def body(moe_input, expert_ids, gate_weights, capacity, gate_proj, up_proj, down_proj, queries, latent_cache, lengths):
    vmem = pl.BlockSpec(memory_space=pltpu.VMEM)
    smem = pl.BlockSpec(memory_space=pltpu.SMEM)
    hbm = pl.BlockSpec(memory_space=pl.ANY)
    widths = [count * LANE for _, count in SUBS]
    per_sub = lambda *lead: [pltpu.VMEM(lead + (w,), BF16) for w in widths]
    dma = lambda *shape: pltpu.SemaphoreType.DMA((2,) + shape)
    scratch = [
        pltpu.VMEM((576, HEADS), BF16), pltpu.VMEM((576, CACHE), BF16),
        pltpu.VMEM((D, HID), BF16), pltpu.VMEM((D, HID), BF16), pltpu.VMEM((HID, D), BF16),
        pltpu.VMEM((HEADS, CACHE), F32), pltpu.VMEM((HEADS, CACHE), BF16),
        pltpu.VMEM((3, 16, FOLD), F32), pltpu.VMEM((3, 4, 16, FOLD), BF16),
        per_sub(3, 2, 256),
        pltpu.VMEM((3, 2, 128, 256), BF16), pltpu.VMEM((256, 1), F32), pltpu.VMEM((256, max(widths)), BF16),
        pltpu.VMEM((256, HID), F32), pltpu.VMEM((256, HID), F32), pltpu.VMEM((3, 2, 256, HID), BF16),
        per_sub(3, 256), per_sub(3, 256), per_sub(3, 6, 32), per_sub(3, 64), per_sub(3, 3, 16),
        pltpu.VMEM((3, 64, FOLD), BF16), pltpu.VMEM((3, 64, FOLD), BF16), pltpu.VMEM((3, 3, 16, FOLD), BF16),
        pltpu.SemaphoreType.DMA((5,)),
        dma(3, 3), dma(3, NSUB, 3), dma(3, NSUB, 4), dma(3, NSUB, 4),
        dma(3, NSUB), dma(3, NSUB, 6), dma(3, NSUB, 3), dma(3, 3),
    ]
    return pl.pallas_call(
        kernel,
        out_shape=(jax.ShapeDtypeStruct((4, D), BF16), jax.ShapeDtypeStruct((1, HEADS, LATENT), BF16)),
        in_specs=[smem, smem, vmem, vmem, vmem, hbm, hbm, hbm, hbm, hbm],
        out_specs=(vmem, vmem),
        scratch_shapes=scratch,
        compiler_params=pltpu.CompilerParams(collective_id=0, has_side_effects=True, vmem_limit_bytes=63 << 20),
        name="fused",
    )(lengths, capacity, moe_input, expert_ids, gate_weights, jnp.swapaxes(queries, 1, 2), jnp.swapaxes(latent_cache, 1, 2), gate_proj, up_proj, down_proj)


def solution(mesh):
    placed = (
        P(("sec", "dev"), None),
        P(("sec", "dev"), None),
        P(("sec", "dev"), None),
        P(),
        P("dev", None, "sec"),
        P("dev", None, "sec"),
        P("dev", "sec", None),
        P(("sec", "dev"), None, None),
        P(("sec", "dev"), None, None),
        P(("sec", "dev")),
    )
    return jax.shard_map(
        body,
        mesh=mesh,
        in_specs=placed,
        out_specs=(P(("sec", "dev"), None), P(("sec", "dev"), None, None)),
        check_vma=False,
    )
```

```python
import functools

import jax
import jax.numpy as jnp
from jax import lax
from jax.experimental import pallas as pl
from jax.experimental.pallas import tpu as pltpu
from jax.sharding import PartitionSpec as P

MESH = pl.DeviceIdType.MESH
BF16 = jnp.bfloat16
F32 = jnp.float32
LATENT = 512
D = 7168
HID = 512
HEADS = 128
CACHE = 2048
EXPERTS = 32
TOP = 8
LANE = 128
PART = 19 * LANE
FOLD = 5 * LANE
SUBS = ((0, 12), (12, 7))
NSUB = len(SUBS)
ORDERS = ("xyz", "yzx", "zxy")
SCALE = 192.0 ** (-0.5)


def span(p, s):
    off, count = SUBS[s]
    skip = LANE if (p == 2 and s == 0) else 0
    start = p * PART + off * LANE + skip - (LANE if p == 2 else 0)
    return skip, count * LANE - skip, start


def mm(a, b):
    return jnp.dot(a, b, preferred_element_type=F32)


def nt(a, b):
    return lax.dot_general(a, b, (((1,), (1,)), ((), ())), preferred_element_type=F32)


def tn(a, b):
    return lax.dot_general(a, b, (((0,), (0,)), ((), ())), preferred_element_type=F32)


def axes_of(i, p):
    a = {ORDERS[p][2]: (i >> 6) & 3, ORDERS[p][1]: (i >> 4) & 3, ORDERS[p][0]: (i >> 2) & 3}
    return a["x"], a["y"], a["z"], (i >> 8) & 1, i & 3


def token_of(i, p):
    x, y, z, c, r = axes_of(i, p)
    return y * 128 + z * 32 + x * 8 + c * 4 + r


def place_of(i, p):
    x, y, z, _, _ = axes_of(i, p)
    return y * 16 + x * 4 + z


def kernel(
    lengths_ref, capacity_ref, x_ref, ids_ref, gw_ref, q_hbm, kv_hbm, gate_hbm, up_hbm, down_hbm,
    out_ref, attn_ref,
    q, kv, gate, up, down, scores, probs,
    fold, s1, xb, sel, sel2, kept_col, packed, acc_g, acc_u, hs, ht,
    cs, cr, tb, rv, us, rw, vq, d3, r3,
    lsem, s1_sem, g2_sem, g3_sem, cx_sem, r0_sem, r1_sem, r2_sem, r3_sem,
):
    y = lax.axis_index("sec")
    dev = lax.axis_index("dev")
    z, x, c = dev // 8, (dev // 2) % 4, dev % 2
    at = {"x": x, "y": y, "z": z}

    def peer(axis, step):
        to = dict(at)
        to[axis] = (at[axis] + step + 4) % 4
        return (to["y"], to["z"] * 8 + to["x"] * 2 + c)

    sibling = (y, z * 8 + x * 2 + (1 - c))
    barrier = pltpu.get_barrier_semaphore()
    for axis in "xyz":
        for step in (1, 2, 3):
            pl.semaphore_signal(barrier, inc=1, device_id=peer(axis, step), device_id_type=MESH)
    pl.semaphore_signal(barrier, inc=1, device_id=sibling, device_id_type=MESH)

    local = {}
    for n, (src, dst) in enumerate(
        ((q_hbm.at[0], q), (kv_hbm.at[0], kv), (gate_hbm.at[0], gate), (up_hbm.at[0], up), (down_hbm.at[0], down))
    ):
        local[n] = pltpu.make_async_copy(src, dst, lsem.at[n])
        local[n].start()

    sent = {}

    def send(key, sems, index, src, dst, to):
        copy = pltpu.make_async_remote_copy(
            src_ref=src, dst_ref=dst,
            send_sem=sems.at[(0,) + index], recv_sem=sems.at[(1,) + index],
            device_id=to, device_id_type=MESH,
        )
        copy.start()
        sent[key] = copy

    def got(key):
        sent[key].wait_recv()

    lane = lax.broadcasted_iota(jnp.int32, (4, LANE), 1)
    info = jnp.zeros((4, LANE), F32)
    ids = ids_ref[...]
    gw = gw_ref[...]
    high = gw.astype(BF16).astype(F32)
    mid = (gw - high).astype(BF16).astype(F32)
    low = gw - high - mid
    for k in range(TOP):
        for n, piece in enumerate((high, mid, low)):
            info = info + jnp.where(lane == ids[:, k:k + 1] + n * EXPERTS, piece[:, k:k + 1], 0.0)
    fold[...] = jnp.zeros_like(fold)
    for p in range(3):
        for f in range(4):
            first, width = f * FOLD, min(FOLD, PART - f * FOLD)
            lead = LANE if (p == 2 and f == 0) else 0
            start = p * PART + first + lead - (LANE if p == 2 else 0)
            fold[p, 4 * f:4 * f + 4, lead:width] = x_ref[:, start:start + width - lead].astype(F32)
    fold[2, 0:4, 0:LANE] = info
    for p in range(3):
        s1[p, at[ORDERS[p][0]]] = fold[p].astype(BF16)
    pl.semaphore_wait(barrier, 10)
    for step in (1, 2, 3):
        for p in range(3):
            axis = ORDERS[p][0]
            mine = s1.at[p, at[axis]]
            send(("s1", p, step), s1_sem, (p, step - 1), mine, mine, peer(axis, step))

    def attend_scores():
        local[0].wait()
        local[1].wait()
        position = lax.broadcasted_iota(jnp.int32, (1, 512), 1)
        length = lengths_ref[0]
        for n in range(CACHE // 512):
            cols = kv[:, n * 512:(n + 1) * 512]
            score = tn(q[:LATENT, :], cols[:LATENT, :]) + tn(q[LATENT:, :], cols[LATENT:, :])
            scores[:, n * 512:(n + 1) * 512] = jnp.where(position + n * 512 < length, score * SCALE, -jnp.inf)

    def attend_probs():
        score = scores[...]
        expo = jnp.exp(score - jnp.max(score, axis=1, keepdims=True))
        probs[...] = (expo / jnp.sum(expo, axis=1, keepdims=True)).astype(BF16)

    def attend_values():
        attn_ref[0] = nt(probs[...], kv[:LATENT, :]).astype(BF16)

    i0 = lax.broadcasted_iota(jnp.int32, (64, 64), 0)
    i1 = lax.broadcasted_iota(jnp.int32, (64, 64), 1)
    turn = jnp.where(((i0 >> 4) == ((i1 >> 2) & 3)) & (((i0 >> 2) & 3) == (i1 >> 4)) & ((i0 & 3) == (i1 & 3)), 1.0, 0.0).astype(BF16)

    def block(p, n, size):
        return pl.ds(pl.multiple_of(n * size, size), size)

    def g2a(p):
        a1, a2, a3 = ORDERS[p]
        for step in (1, 2, 3):
            got(("s1", p, step))
        rows = mm(turn, s1[p].reshape(64, FOLD)).astype(BF16)
        own = block(p, at[a3] * 4 + at[a2], 16)
        for f in range(4):
            for t in range(5):
                tile = 5 * f + t
                for s, (off, count) in enumerate(SUBS):
                    if off <= tile < off + count:
                        xb[s][p, c, own, (tile - off) * LANE:(tile - off + 1) * LANE] = rows[16 * f:16 * f + 16, t * LANE:(t + 1) * LANE]
        for s in range(NSUB):
            ref = xb[s].at[p, c, own]
            send(("g2", p, s, 0), g2_sem, (p, s, 0), ref, ref, peer(a2, 1))
            send(("g2", p, s, 1), g2_sem, (p, s, 1), ref, ref, peer(a2, -1))

    def g2b(p, s):
        _, a2, a3 = ORDERS[p]
        way = 0 if (p + s) % 2 == 0 else 1
        got(("g2", p, s, way))
        off = -1 if way == 0 else 1
        ref = xb[s].at[p, c, block(p, at[a3] * 4 + (at[a2] + off + 4) % 4, 16)]
        send(("g2", p, s, 2), g2_sem, (p, s, 2), ref, ref, peer(a2, -off))

    def g3a(p, s):
        _, a2, a3 = ORDERS[p]
        way = 0 if (p + s) % 2 == 0 else 1
        got(("g2", p, s, 1 - way))
        got(("g2", p, s, 2))
        ref = xb[s].at[p, c, block(p, at[a3], 64)]
        send(("g3", p, s, 0), g3_sem, (p, s, 0), ref, ref, peer(a3, 1))
        send(("g3", p, s, 1), g3_sem, (p, s, 1), ref, ref, peer(a3, -1))
        send(("cx", p, s, 0), cx_sem, (p, s, 0), ref, ref, sibling)

    def g3b(p, s):
        a3 = ORDERS[p][2]
        for way, off in ((0, -1), (1, 1)):
            got(("g3", p, s, way))
            whole = (at[a3] + off + 4) % 4
            ref = xb[s].at[p, c, block(p, whole * 2 + way, 32)]
            send(("g3", p, s, 2 + way), g3_sem, (p, s, 2 + way), ref, ref, peer(a3, -off))
            ref = xb[s].at[p, c, block(p, whole, 64)]
            send(("cx", p, s, 1 + way), cx_sem, (p, s, 1 + way), ref, ref, sibling)

    def g3c(p, s):
        a3 = ORDERS[p][2]
        got(("g3", p, s, 2))
        got(("g3", p, s, 3))
        ref = xb[s].at[p, c, block(p, (at[a3] + 2) % 4, 64)]
        send(("cx", p, s, 3), cx_sem, (p, s, 3), ref, ref, sibling)

    def cxw(p, s):
        for n in range(4):
            got(("cx", p, s, n))

    def routing():
        pick = lax.broadcasted_iota(jnp.int32, (8, LANE), 1)
        which = lax.broadcasted_iota(jnp.int32, (8, LANE), 0)
        expert = jnp.where(which == 0, dev, dev + 1 - 2 * c)
        pick = jnp.where((pick < 3 * EXPERTS) & ((pick & (EXPERTS - 1)) == expert), 1.0, 0.0).astype(BF16)
        weight = jnp.concatenate([nt(pick, xb[0][2, cc, :, 0:LANE]) for cc in range(2)], axis=1)
        named = weight > 0.0
        flag = jnp.where(named, 1.0, 0.0).astype(BF16)
        rows = lax.broadcasted_iota(jnp.int32, (512, 1), 0)
        cols = lax.broadcasted_iota(jnp.int32, (1, 512), 1)
        ones = lambda cond: jnp.where(cond, 1.0, 0.0).astype(BF16)
        arrival = mm(flag, ones(token_of(rows, 2) < token_of(cols, 2)))
        rank = mm(flag, ones(((rows >> 2) == (cols >> 2)) & (rows < cols)))
        limit = capacity_ref[dev].astype(F32)
        kept = jnp.where(arrival < limit, weight, 0.0)
        code = jnp.where(named, rank + 1.0, 0.0)
        for p in range(3):
            turned = code if p == 2 else mm(code.astype(BF16), ones(token_of(rows, 2) == token_of(cols, p)))
            for cc in range(2):
                slot = lax.broadcasted_iota(jnp.int32, (128, 1), 0)
                row = lax.broadcasted_iota(jnp.int32, (1, 256), 1)
                wanted = ((slot & 1) + 1).astype(F32)
                chosen = ((slot >> 1) == place_of(row, p)) & (turned[0:1, cc * 256:(cc + 1) * 256] == wanted)
                sel[p, cc] = ones(chosen)
                other = (slot >> 1 == place_of(row, p)) & (turned[1:2, cc * 256:(cc + 1) * 256] == wanted)
                sel2[p, cc] = ones(other)
                if p == 2:
                    kept_col[cc * 128:(cc + 1) * 128, :] = jnp.sum(
                        jnp.where(chosen, kept[0:1, cc * 256:(cc + 1) * 256], 0.0), axis=1, keepdims=True)

    def ffn(p, s):
        skip, width, start = span(p, s)
        for cc in range(2):
            packed[cc * 128:(cc + 1) * 128, :width] = mm(sel[p, cc], xb[s][p, cc, :, skip:skip + width]).astype(BF16)
        rows = packed[:, :width]
        acc_g[...] += mm(rows, gate[start:start + width, :])
        acc_u[...] += mm(rows, up[start:start + width, :])

    def act():
        g = acc_g[...]
        hidden = (g * (1.0 / (1.0 + jnp.exp(-g))) * acc_u[...] * kept_col[...]).astype(BF16)
        hs[...] = hidden.reshape(2, 128, HID)

    def spread():
        for p in range(3):
            ht[p] = tn(sel[p, c], hs[c]).astype(BF16)

    def c0(p, s):
        _, width, start = span(p, s)
        cs[s][p, :, :width] = mm(hs[1 - c], down[:, start:start + width]).astype(BF16)
        send(("r0", p, s), r0_sem, (p, s), cs[s].at[p, :, :width], cr[s].at[p, :, :width], sibling)

    def plus(ref, rows, width, *others):
        total = ref[rows, :width].astype(F32)
        for other in others:
            total = total + other[:, :width].astype(F32)
        return total.astype(BF16)

    def a1(p, s):
        _, width, start = span(p, s)
        mine = mm(ht[p], down[:, start:start + width])
        got(("r0", p, s))
        tb[s][p, :, :width] = (mine + tn(sel2[p, c], cr[s][p, :, :width])).astype(BF16)
        axis = ORDERS[p][2]
        k = at[axis]
        for n, (off, half, way) in enumerate(((2, 0, 1), (2, 1, -1), (1, 1, 1), (-1, 0, -1))):
            rows = block(p, ((k + off + 4) % 4) * 2 + half, 32)
            send(("r1", p, s, n), r1_sem, (p, s, n), tb[s].at[p, rows, :width], rv[s].at[p, n, :, :width], peer(axis, way))

    def a2(p, s):
        _, width, _ = span(p, s)
        axis = ORDERS[p][2]
        k = at[axis]
        for n, (off, half, way) in enumerate(((1, 0, 1), (-1, 1, -1))):
            got(("r1", p, s, n))
            rows = block(p, ((k + off + 4) % 4) * 2 + half, 32)
            t = tb[s].at[p]
            t[rows, :width] = plus(t, rows, width, rv[s].at[p, n])
            send(("r1", p, s, 4 + n), r1_sem, (p, s, 4 + n), tb[s].at[p, rows, :width], rv[s].at[p, 4 + n, :, :width], peer(axis, way))

    def b1(p, s):
        _, width, _ = span(p, s)
        k = at[ORDERS[p][2]]
        for n in (2, 3, 4, 5):
            got(("r1", p, s, n))
        t, u, v = tb[s].at[p], us[s].at[p], rv[s].at[p]
        u[0:32, :width] = plus(t, block(p, k * 2, 32), width, v.at[3], v.at[4])
        u[32:64, :width] = plus(t, block(p, k * 2 + 1, 32), width, v.at[2], v.at[5])
        axis = ORDERS[p][1]
        k = at[axis]
        way = 1 if (p + s) % 2 == 0 else -1
        for n, (off, to) in enumerate(((2, way), (-way, -way))):
            rows = block(p, (k + off + 4) % 4, 16)
            send(("r2", p, s, n), r2_sem, (p, s, n), u.at[rows, :width], rw[s].at[p, n, :, :width], peer(axis, to))

    def b2(p, s):
        _, width, _ = span(p, s)
        axis = ORDERS[p][1]
        k = at[axis]
        way = 1 if (p + s) % 2 == 0 else -1
        got(("r2", p, s, 0))
        rows = block(p, (k + way + 4) % 4, 16)
        u = us[s].at[p]
        u[rows, :width] = plus(u, rows, width, rw[s].at[p, 0])
        send(("r2", p, s, 2), r2_sem, (p, s, 2), u.at[rows, :width], rw[s].at[p, 2, :, :width], peer(axis, way))

    def b3(p, s):
        skip, width, _ = span(p, s)
        k = at[ORDERS[p][1]]
        got(("r2", p, s, 1))
        got(("r2", p, s, 2))
        total = plus(us[s].at[p], block(p, k, 16), width, rw[s].at[p, 1], rw[s].at[p, 2])
        off = SUBS[s][0]
        for t in range(width // LANE):
            tile = off + skip // LANE + t
            f, j = tile // 5, tile % 5
            vq[p, 16 * f:16 * f + 16, j * LANE:(j + 1) * LANE] = total[:, t * LANE:(t + 1) * LANE]

    def r3a(p):
        axis = ORDERS[p][0]
        d3[p] = mm(turn, vq[p]).astype(BF16)
        for step in (1, 2, 3):
            rows = block(p, (at[axis] + step) % 4, 16)
            send(("r3", p, step), r3_sem, (p, step - 1), d3.at[p, rows], r3.at[p, step - 1], peer(axis, step))

    def r3b(p):
        axis = ORDERS[p][0]
        total = d3[p, block(p, at[axis], 16), :].astype(F32)
        for step in (1, 2, 3):
            got(("r3", p, step))
            total = total + r3[p, step - 1].astype(F32)
        fold[p] = total
        for f in range(4):
            first, width = f * FOLD, min(FOLD, PART - f * FOLD)
            lead = LANE if (p == 2 and f == 0) else 0
            start = p * PART + first + lead - (LANE if p == 2 else 0)
            out_ref[:, start:start + width - lead] = fold[p, 4 * f:4 * f + 4, lead:width].astype(BF16)

    every = lambda step, *rest: [step(p, *rest) for p in range(3)]
    acc_g[...] = jnp.zeros_like(acc_g)
    acc_u[...] = jnp.zeros_like(acc_u)
    vq[...] = jnp.zeros_like(vq)
    every(g2a)
    for s in range(NSUB):
        every(g2b, s)
    for s in range(NSUB):
        every(g3a, s)
    attend_scores()
    attend_probs()
    attend_values()
    for s in range(NSUB):
        every(g3b, s)
    for s in range(NSUB):
        every(g3c, s)
    every(cxw, 0)
    routing()
    local[2].wait()
    local[3].wait()
    every(ffn, 0)
    every(cxw, 1)
    every(ffn, 1)
    act()
    local[4].wait()
    every(c0, 1)
    every(c0, 0)
    spread()
    for stage in (a1, a2, b1, b2, b3):
        every(stage, 1)
        every(stage, 0)
    every(r3a)
    every(r3b)
    for copy in sent.values():
        copy.wait_send()


def body(moe_input, expert_ids, gate_weights, capacity, gate_proj, up_proj, down_proj, queries, latent_cache, lengths):
    vmem = pl.BlockSpec(memory_space=pltpu.VMEM)
    smem = pl.BlockSpec(memory_space=pltpu.SMEM)
    hbm = pl.BlockSpec(memory_space=pl.ANY)
    widths = [count * LANE for _, count in SUBS]
    per_sub = lambda *lead: [pltpu.VMEM(lead + (w,), BF16) for w in widths]
    dma = lambda *shape: pltpu.SemaphoreType.DMA((2,) + shape)
    scratch = [
        pltpu.VMEM((576, HEADS), BF16), pltpu.VMEM((576, CACHE), BF16),
        pltpu.VMEM((D, HID), BF16), pltpu.VMEM((D, HID), BF16), pltpu.VMEM((HID, D), BF16),
        pltpu.VMEM((HEADS, CACHE), F32), pltpu.VMEM((HEADS, CACHE), BF16),
        pltpu.VMEM((3, 16, FOLD), F32), pltpu.VMEM((3, 4, 16, FOLD), BF16),
        per_sub(3, 2, 256),
        pltpu.VMEM((3, 2, 128, 256), BF16), pltpu.VMEM((3, 2, 128, 256), BF16), pltpu.VMEM((256, 1), F32), pltpu.VMEM((256, max(widths)), BF16),
        pltpu.VMEM((256, HID), F32), pltpu.VMEM((256, HID), F32), pltpu.VMEM((2, 128, HID), BF16), pltpu.VMEM((3, 256, HID), BF16),
        per_sub(3, 128), per_sub(3, 128), per_sub(3, 256), per_sub(3, 6, 32), per_sub(3, 64), per_sub(3, 3, 16),
        pltpu.VMEM((3, 64, FOLD), BF16), pltpu.VMEM((3, 64, FOLD), BF16), pltpu.VMEM((3, 3, 16, FOLD), BF16),
        pltpu.SemaphoreType.DMA((5,)),
        dma(3, 3), dma(3, NSUB, 3), dma(3, NSUB, 4), dma(3, NSUB, 4),
        dma(3, NSUB), dma(3, NSUB, 6), dma(3, NSUB, 3), dma(3, 3),
    ]
    return pl.pallas_call(
        kernel,
        out_shape=(jax.ShapeDtypeStruct((4, D), BF16), jax.ShapeDtypeStruct((1, HEADS, LATENT), BF16)),
        in_specs=[smem, smem, vmem, vmem, vmem, hbm, hbm, hbm, hbm, hbm],
        out_specs=(vmem, vmem),
        scratch_shapes=scratch,
        compiler_params=pltpu.CompilerParams(collective_id=0, has_side_effects=True, vmem_limit_bytes=63 << 20),
        name="fused",
    )(lengths, capacity, moe_input, expert_ids, gate_weights, jnp.swapaxes(queries, 1, 2), jnp.swapaxes(latent_cache, 1, 2), gate_proj, up_proj, down_proj)


def solution(mesh):
    placed = (
        P(("sec", "dev"), None),
        P(("sec", "dev"), None),
        P(("sec", "dev"), None),
        P(),
        P("dev", None, "sec"),
        P("dev", None, "sec"),
        P("dev", "sec", None),
        P(("sec", "dev"), None, None),
        P(("sec", "dev"), None, None),
        P(("sec", "dev")),
    )
    return jax.shard_map(
        body,
        mesh=mesh,
        in_specs=placed,
        out_specs=(P(("sec", "dev"), None), P(("sec", "dev"), None, None)),
        check_vma=False,
    )
```

```python
import functools

import jax
import jax.numpy as jnp
from jax import lax
from jax.experimental import pallas as pl
from jax.experimental.pallas import tpu as pltpu
from jax.sharding import PartitionSpec as P

MESH = pl.DeviceIdType.MESH
BF16 = jnp.bfloat16
F32 = jnp.float32
LATENT = 512
D = 7168
HID = 512
HEADS = 128
CACHE = 2048
EXPERTS = 32
TOP = 8
LANE = 128
PART = 19 * LANE
FOLD = 5 * LANE
SUBS = ((0, 12), (12, 7))
NSUB = len(SUBS)
ORDERS = ("xyz", "yzx", "zxy")
SCALE = 192.0 ** (-0.5)


def span(p, s):
    off, count = SUBS[s]
    skip = LANE if (p == 2 and s == 0) else 0
    start = p * PART + off * LANE + skip - (LANE if p == 2 else 0)
    return skip, count * LANE - skip, start


def mm(a, b):
    return jnp.dot(a, b, preferred_element_type=F32)


def nt(a, b):
    return lax.dot_general(a, b, (((1,), (1,)), ((), ())), preferred_element_type=F32)


def tn(a, b):
    return lax.dot_general(a, b, (((0,), (0,)), ((), ())), preferred_element_type=F32)


def axes_of(i, p):
    a = {ORDERS[p][2]: (i >> 6) & 3, ORDERS[p][1]: (i >> 4) & 3, ORDERS[p][0]: (i >> 2) & 3}
    return a["x"], a["y"], a["z"], (i >> 8) & 1, i & 3


def token_of(i, p):
    x, y, z, c, r = axes_of(i, p)
    return y * 128 + z * 32 + x * 8 + c * 4 + r


def place_of(i, p):
    x, y, z, _, _ = axes_of(i, p)
    return y * 16 + x * 4 + z


def kernel(
    lengths_ref, capacity_ref, x_hbm, ids_hbm, gw_hbm, q_hbm, kv_hbm, gate_hbm, up_hbm, down_hbm,
    out_ref, attn_ref,
    x_ref, ids_ref, gw_ref, q, kv, gate, up, down, scores, probs, masks,
    fold, s1, xb, sel, sel2, kept_col, packed, acc_g, acc_u, hs, ht,
    cs, cr, tb, rv, us, rw, vq, d3, r3,
    lsem, s1_sem, g2_sem, g3_sem, cx_sem, r0_sem, r1_sem, r2_sem, r3_sem,
):
    y = lax.axis_index("sec")
    dev = lax.axis_index("dev")
    z, x, c = dev // 8, (dev // 2) % 4, dev % 2
    at = {"x": x, "y": y, "z": z}

    def peer(axis, step):
        to = dict(at)
        to[axis] = (at[axis] + step + 4) % 4
        return (to["y"], to["z"] * 8 + to["x"] * 2 + c)

    sibling = (y, z * 8 + x * 2 + (1 - c))
    barrier = pltpu.get_barrier_semaphore()
    for axis in "xyz":
        for step in (1, 2, 3):
            pl.semaphore_signal(barrier, inc=1, device_id=peer(axis, step), device_id_type=MESH)
    pl.semaphore_signal(barrier, inc=1, device_id=sibling, device_id_type=MESH)

    small = []
    for n, (src, dst) in enumerate(((x_hbm, x_ref), (ids_hbm, ids_ref), (gw_hbm, gw_ref))):
        small.append(pltpu.make_async_copy(src, dst, lsem.at[5 + n]))
        small[n].start()
    local = {}
    for n, (src, dst) in enumerate(
        ((q_hbm.at[0], q), (kv_hbm.at[0], kv), (gate_hbm.at[0], gate), (up_hbm.at[0], up), (down_hbm.at[0], down))
    ):
        local[n] = pltpu.make_async_copy(src, dst, lsem.at[n])
        local[n].start()

    sent = {}

    def send(key, sems, index, src, dst, to):
        copy = pltpu.make_async_remote_copy(
            src_ref=src, dst_ref=dst,
            send_sem=sems.at[(0,) + index], recv_sem=sems.at[(1,) + index],
            device_id=to, device_id_type=MESH,
        )
        copy.start()
        sent[key] = copy

    def got(key):
        sent[key].wait_recv()

    for copy in small:
        copy.wait()
    def drain(*kinds):
        for key, copy in sent.items():
            if key[0] in kinds:
                copy.wait_send()

    lane = lax.broadcasted_iota(jnp.int32, (4, LANE), 1)
    info = jnp.zeros((4, LANE), F32)
    ids = ids_ref[...]
    gw = gw_ref[...]
    high = gw.astype(BF16).astype(F32)
    mid = (gw - high).astype(BF16).astype(F32)
    low = gw - high - mid
    for k in range(TOP):
        for n, piece in enumerate((high, mid, low)):
            info = info + jnp.where(lane == ids[:, k:k + 1] + n * EXPERTS, piece[:, k:k + 1], 0.0)
    fold[...] = jnp.zeros_like(fold)
    for p in range(3):
        for f in range(4):
            first, width = f * FOLD, min(FOLD, PART - f * FOLD)
            lead = LANE if (p == 2 and f == 0) else 0
            start = p * PART + first + lead - (LANE if p == 2 else 0)
            fold[p, 4 * f:4 * f + 4, lead:width] = x_ref[:, start:start + width - lead].astype(F32)
    fold[2, 0:4, 0:LANE] = info
    for p in range(3):
        s1[p, at[ORDERS[p][0]]] = fold[p].astype(BF16)
    pl.semaphore_wait(barrier, 10)
    for step in (1, 2, 3):
        for p in range(3):
            axis = ORDERS[p][0]
            mine = s1.at[p, at[axis]]
            send(("s1", p, step), s1_sem, (p, step - 1), mine, mine, peer(axis, step))

    def attend_scores():
        local[0].wait()
        local[1].wait()
        position = lax.broadcasted_iota(jnp.int32, (1, 512), 1)
        length = lengths_ref[0]
        for n in range(CACHE // 512):
            cols = kv[:, n * 512:(n + 1) * 512]
            score = tn(q[:LATENT, :], cols[:LATENT, :]) + tn(q[LATENT:, :], cols[LATENT:, :])
            scores[:, n * 512:(n + 1) * 512] = jnp.where(position + n * 512 < length, score * SCALE, -jnp.inf)

    def attend_probs():
        score = scores[...]
        expo = jnp.exp(score - jnp.max(score, axis=1, keepdims=True))
        probs[...] = (expo / jnp.sum(expo, axis=1, keepdims=True)).astype(BF16)

    def attend_values():
        attn_ref[0] = nt(probs[...], kv[:LATENT, :]).astype(BF16)

    i0 = lax.broadcasted_iota(jnp.int32, (64, 64), 0)
    i1 = lax.broadcasted_iota(jnp.int32, (64, 64), 1)
    turn = jnp.where(((i0 >> 4) == ((i1 >> 2) & 3)) & (((i0 >> 2) & 3) == (i1 >> 4)) & ((i0 & 3) == (i1 & 3)), 1.0, 0.0).astype(BF16)

    def block(p, n, size):
        return pl.ds(pl.multiple_of(n * size, size), size)

    def g2a(p):
        a1, a2, a3 = ORDERS[p]
        for step in (1, 2, 3):
            got(("s1", p, step))
        rows = mm(turn, s1[p].reshape(64, FOLD)).astype(BF16)
        own = block(p, at[a3] * 4 + at[a2], 16)
        for f in range(4):
            for t in range(5):
                tile = 5 * f + t
                for s, (off, count) in enumerate(SUBS):
                    if off <= tile < off + count:
                        xb[s][p, c, own, (tile - off) * LANE:(tile - off + 1) * LANE] = rows[16 * f:16 * f + 16, t * LANE:(t + 1) * LANE]
        for s in range(NSUB):
            ref = xb[s].at[p, c, own]
            send(("g2", p, s, 0), g2_sem, (p, s, 0), ref, ref, peer(a2, 1))
            send(("g2", p, s, 1), g2_sem, (p, s, 1), ref, ref, peer(a2, -1))

    def g2b(p, s):
        _, a2, a3 = ORDERS[p]
        way = 0 if (p + s) % 2 == 0 else 1
        got(("g2", p, s, way))
        off = -1 if way == 0 else 1
        ref = xb[s].at[p, c, block(p, at[a3] * 4 + (at[a2] + off + 4) % 4, 16)]
        send(("g2", p, s, 2), g2_sem, (p, s, 2), ref, ref, peer(a2, -off))

    def g3a(p, s):
        _, a2, a3 = ORDERS[p]
        way = 0 if (p + s) % 2 == 0 else 1
        got(("g2", p, s, 1 - way))
        got(("g2", p, s, 2))
        ref = xb[s].at[p, c, block(p, at[a3], 64)]
        send(("g3", p, s, 0), g3_sem, (p, s, 0), ref, ref, peer(a3, 1))
        send(("g3", p, s, 1), g3_sem, (p, s, 1), ref, ref, peer(a3, -1))
        send(("cx", p, s, 0), cx_sem, (p, s, 0), ref, ref, sibling)

    def g3b(p, s):
        a3 = ORDERS[p][2]
        for way, off in ((0, -1), (1, 1)):
            got(("g3", p, s, way))
            whole = (at[a3] + off + 4) % 4
            ref = xb[s].at[p, c, block(p, whole * 2 + way, 32)]
            send(("g3", p, s, 2 + way), g3_sem, (p, s, 2 + way), ref, ref, peer(a3, -off))
            ref = xb[s].at[p, c, block(p, whole, 64)]
            send(("cx", p, s, 1 + way), cx_sem, (p, s, 1 + way), ref, ref, sibling)

    def g3c(p, s):
        a3 = ORDERS[p][2]
        got(("g3", p, s, 2))
        got(("g3", p, s, 3))
        ref = xb[s].at[p, c, block(p, (at[a3] + 2) % 4, 64)]
        send(("cx", p, s, 3), cx_sem, (p, s, 3), ref, ref, sibling)

    def cxw(p, s):
        for n in range(4):
            got(("cx", p, s, n))

    ones = lambda cond: jnp.where(cond, 1.0, 0.0).astype(BF16)

    def orders():
        rows = lax.broadcasted_iota(jnp.int32, (512, 1), 0)
        cols = lax.broadcasted_iota(jnp.int32, (1, 512), 1)
        masks[0] = ones(token_of(rows, 2) == token_of(cols, 0))
        masks[1] = ones(token_of(rows, 2) == token_of(cols, 1))
        masks[2] = ones(token_of(rows, 2) < token_of(cols, 2))
        masks[3] = ones(((rows >> 2) == (cols >> 2)) & (rows < cols))

    def routing():
        pick = lax.broadcasted_iota(jnp.int32, (8, LANE), 1)
        which = lax.broadcasted_iota(jnp.int32, (8, LANE), 0)
        expert = jnp.where(which == 0, dev, dev + 1 - 2 * c)
        pick = jnp.where((pick < 3 * EXPERTS) & ((pick & (EXPERTS - 1)) == expert), 1.0, 0.0).astype(BF16)
        weight = jnp.concatenate([nt(pick, xb[0][2, cc, :, 0:LANE]) for cc in range(2)], axis=1)
        named = weight > 0.0
        flag = jnp.where(named, 1.0, 0.0).astype(BF16)
        arrival = mm(flag, masks[2])
        rank = mm(flag, masks[3])
        limit = capacity_ref[dev].astype(F32)
        kept = jnp.where(arrival < limit, weight, 0.0)
        code = jnp.where(named, rank + 1.0, 0.0)
        for p in range(3):
            turned = code if p == 2 else mm(code.astype(BF16), masks[p])
            for cc in range(2):
                slot = lax.broadcasted_iota(jnp.int32, (128, 1), 0)
                row = lax.broadcasted_iota(jnp.int32, (1, 256), 1)
                wanted = ((slot & 1) + 1).astype(F32)
                chosen = ((slot >> 1) == place_of(row, p)) & (turned[0:1, cc * 256:(cc + 1) * 256] == wanted)
                sel[p, cc] = ones(chosen)
                other = (slot >> 1 == place_of(row, p)) & (turned[1:2, cc * 256:(cc + 1) * 256] == wanted)
                sel2[p, cc] = ones(other)
                if p == 2:
                    kept_col[cc * 128:(cc + 1) * 128, :] = jnp.sum(
                        jnp.where(chosen, kept[0:1, cc * 256:(cc + 1) * 256], 0.0), axis=1, keepdims=True)

    def ffn(p, s):
        skip, width, start = span(p, s)
        for cc in range(2):
            packed[cc * 128:(cc + 1) * 128, :width] = mm(sel[p, cc], xb[s][p, cc, :, skip:skip + width]).astype(BF16)
        rows = packed[:, :width]
        acc_g[...] += mm(rows, gate[start:start + width, :])
        acc_u[...] += mm(rows, up[start:start + width, :])

    def act():
        g = acc_g[...]
        hidden = (g * (1.0 / (1.0 + jnp.exp(-g))) * acc_u[...] * kept_col[...]).astype(BF16)
        hs[...] = hidden.reshape(2, 128, HID)

    def spread():
        for p in range(3):
            ht[p] = tn(sel[p, c], hs[c]).astype(BF16)

    def c0(p, s):
        _, width, start = span(p, s)
        cs[s][p, :, :width] = mm(hs[1 - c], down[:, start:start + width]).astype(BF16)
        send(("r0", p, s), r0_sem, (p, s), cs[s].at[p, :, :width], cr[s].at[p, :, :width], sibling)

    def plus(ref, rows, width, *others):
        total = ref[rows, :width].astype(F32)
        for other in others:
            total = total + other[:, :width].astype(F32)
        return total.astype(BF16)

    def a1(p, s):
        _, width, start = span(p, s)
        mine = mm(ht[p], down[:, start:start + width])
        got(("r0", p, s))
        tb[s][p, :, :width] = (mine + tn(sel2[p, c], cr[s][p, :, :width])).astype(BF16)
        axis = ORDERS[p][2]
        k = at[axis]
        for n, (off, half, way) in enumerate(((2, 0, 1), (2, 1, -1), (1, 1, 1), (-1, 0, -1))):
            rows = block(p, ((k + off + 4) % 4) * 2 + half, 32)
            send(("r1", p, s, n), r1_sem, (p, s, n), tb[s].at[p, rows, :width], rv[s].at[p, n, :, :width], peer(axis, way))

    def a2(p, s):
        _, width, _ = span(p, s)
        axis = ORDERS[p][2]
        k = at[axis]
        for n, (off, half, way) in enumerate(((1, 0, 1), (-1, 1, -1))):
            got(("r1", p, s, n))
            rows = block(p, ((k + off + 4) % 4) * 2 + half, 32)
            t = tb[s].at[p]
            t[rows, :width] = plus(t, rows, width, rv[s].at[p, n])
            send(("r1", p, s, 4 + n), r1_sem, (p, s, 4 + n), tb[s].at[p, rows, :width], rv[s].at[p, 4 + n, :, :width], peer(axis, way))

    def b1(p, s):
        _, width, _ = span(p, s)
        k = at[ORDERS[p][2]]
        for n in (2, 3, 4, 5):
            got(("r1", p, s, n))
        t, u, v = tb[s].at[p], us[s].at[p], rv[s].at[p]
        u[0:32, :width] = plus(t, block(p, k * 2, 32), width, v.at[3], v.at[4])
        u[32:64, :width] = plus(t, block(p, k * 2 + 1, 32), width, v.at[2], v.at[5])
        axis = ORDERS[p][1]
        k = at[axis]
        way = 1 if (p + s) % 2 == 0 else -1
        for n, (off, to) in enumerate(((2, way), (-way, -way))):
            rows = block(p, (k + off + 4) % 4, 16)
            send(("r2", p, s, n), r2_sem, (p, s, n), u.at[rows, :width], rw[s].at[p, n, :, :width], peer(axis, to))

    def b2(p, s):
        _, width, _ = span(p, s)
        axis = ORDERS[p][1]
        k = at[axis]
        way = 1 if (p + s) % 2 == 0 else -1
        got(("r2", p, s, 0))
        rows = block(p, (k + way + 4) % 4, 16)
        u = us[s].at[p]
        u[rows, :width] = plus(u, rows, width, rw[s].at[p, 0])
        send(("r2", p, s, 2), r2_sem, (p, s, 2), u.at[rows, :width], rw[s].at[p, 2, :, :width], peer(axis, way))

    def b3(p, s):
        skip, width, _ = span(p, s)
        k = at[ORDERS[p][1]]
        got(("r2", p, s, 1))
        got(("r2", p, s, 2))
        total = plus(us[s].at[p], block(p, k, 16), width, rw[s].at[p, 1], rw[s].at[p, 2])
        off = SUBS[s][0]
        for t in range(width // LANE):
            tile = off + skip // LANE + t
            f, j = tile // 5, tile % 5
            vq[p, 16 * f:16 * f + 16, j * LANE:(j + 1) * LANE] = total[:, t * LANE:(t + 1) * LANE]

    def r3a(p):
        axis = ORDERS[p][0]
        d3[p] = mm(turn, vq[p]).astype(BF16)
        for step in (1, 2, 3):
            rows = block(p, (at[axis] + step) % 4, 16)
            send(("r3", p, step), r3_sem, (p, step - 1), d3.at[p, rows], r3.at[p, step - 1], peer(axis, step))

    def r3b(p):
        axis = ORDERS[p][0]
        total = d3[p, block(p, at[axis], 16), :].astype(F32)
        for step in (1, 2, 3):
            got(("r3", p, step))
            total = total + r3[p, step - 1].astype(F32)
        fold[p] = total
        for f in range(4):
            first, width = f * FOLD, min(FOLD, PART - f * FOLD)
            lead = LANE if (p == 2 and f == 0) else 0
            start = p * PART + first + lead - (LANE if p == 2 else 0)
            out_ref[:, start:start + width - lead] = fold[p, 4 * f:4 * f + 4, lead:width].astype(BF16)

    every = lambda step, *rest: [step(p, *rest) for p in range(3)]
    acc_g[...] = jnp.zeros_like(acc_g)
    acc_u[...] = jnp.zeros_like(acc_u)
    vq[...] = jnp.zeros_like(vq)
    every(g2a)
    for s in range(NSUB):
        every(g2b, s)
    for s in range(NSUB):
        every(g3a, s)
    attend_scores()
    attend_probs()
    attend_values()
    orders()
    for s in range(NSUB):
        every(g3b, s)
    for s in range(NSUB):
        every(g3c, s)
    every(cxw, 0)
    routing()
    local[2].wait()
    local[3].wait()
    every(ffn, 0)
    every(cxw, 1)
    every(ffn, 1)
    act()
    local[4].wait()
    every(c0, 1)
    every(c0, 0)
    spread()
    every(a1, 1)
    every(a1, 0)
    drain("s1", "g2", "g3", "cx")
    for stage in (a2, b1, b2, b3):
        every(stage, 1)
        every(stage, 0)
    every(r3a)
    drain("r0", "r1", "r2")
    every(r3b)
    drain("r3")


def store(mixed, attended, mixed_out, attended_out, sem):
    copies = [
        pltpu.make_async_copy(mixed, mixed_out, sem.at[0]),
        pltpu.make_async_copy(attended, attended_out, sem.at[1]),
    ]
    for copy in copies:
        copy.start()
    for copy in copies:
        copy.wait()


def body(moe_input, expert_ids, gate_weights, capacity, gate_proj, up_proj, down_proj, queries, latent_cache, lengths):
    vmem = pl.BlockSpec(memory_space=pltpu.VMEM)
    smem = pl.BlockSpec(memory_space=pltpu.SMEM)
    hbm = pl.BlockSpec(memory_space=pl.ANY)
    widths = [count * LANE for _, count in SUBS]
    per_sub = lambda *lead: [pltpu.VMEM(lead + (w,), BF16) for w in widths]
    dma = lambda *shape: pltpu.SemaphoreType.DMA((2,) + shape)
    scratch = [
        pltpu.VMEM((4, D), BF16), pltpu.VMEM((4, TOP), jnp.int32), pltpu.VMEM((4, TOP), F32),
        pltpu.VMEM((576, HEADS), BF16), pltpu.VMEM((576, CACHE), BF16),
        pltpu.VMEM((D, HID), BF16), pltpu.VMEM((D, HID), BF16), pltpu.VMEM((HID, D), BF16),
        pltpu.VMEM((HEADS, CACHE), F32), pltpu.VMEM((HEADS, CACHE), BF16), pltpu.VMEM((4, 512, 512), BF16),
        pltpu.VMEM((3, 16, FOLD), F32), pltpu.VMEM((3, 4, 16, FOLD), BF16),
        per_sub(3, 2, 256),
        pltpu.VMEM((3, 2, 128, 256), BF16), pltpu.VMEM((3, 2, 128, 256), BF16), pltpu.VMEM((256, 1), F32), pltpu.VMEM((256, max(widths)), BF16),
        pltpu.VMEM((256, HID), F32), pltpu.VMEM((256, HID), F32), pltpu.VMEM((2, 128, HID), BF16), pltpu.VMEM((3, 256, HID), BF16),
        per_sub(3, 128), per_sub(3, 128), per_sub(3, 256), per_sub(3, 6, 32), per_sub(3, 64), per_sub(3, 3, 16),
        pltpu.VMEM((3, 64, FOLD), BF16), pltpu.VMEM((3, 64, FOLD), BF16), pltpu.VMEM((3, 3, 16, FOLD), BF16),
        pltpu.SemaphoreType.DMA((8,)),
        dma(3, 3), dma(3, NSUB, 3), dma(3, NSUB, 4), dma(3, NSUB, 4),
        dma(3, NSUB), dma(3, NSUB, 6), dma(3, NSUB, 3), dma(3, 3),
    ]
    mixed, attended = pl.pallas_call(
        kernel,
        out_shape=(jax.ShapeDtypeStruct((4, D), BF16), jax.ShapeDtypeStruct((1, HEADS, LATENT), BF16)),
        in_specs=[smem, smem, hbm, hbm, hbm, hbm, hbm, hbm, hbm, hbm],
        out_specs=(vmem, vmem),
        scratch_shapes=scratch,
        compiler_params=pltpu.CompilerParams(collective_id=0, has_side_effects=True, vmem_limit_bytes=63 << 20),
        name="fused",
    )(lengths, capacity, moe_input, expert_ids, gate_weights, jnp.swapaxes(queries, 1, 2), jnp.swapaxes(latent_cache, 1, 2), gate_proj, up_proj, down_proj)
    return pl.pallas_call(
        store,
        out_shape=(jax.ShapeDtypeStruct((4, D), BF16), jax.ShapeDtypeStruct((1, HEADS, LATENT), BF16)),
        in_specs=[hbm, hbm],
        out_specs=(hbm, hbm),
        scratch_shapes=[pltpu.SemaphoreType.DMA((2,))],
        compiler_params=pltpu.CompilerParams(vmem_limit_bytes=62 << 20),
        name="store",
    )(mixed, attended)


def solution(mesh):
    placed = (
        P(("sec", "dev"), None),
        P(("sec", "dev"), None),
        P(("sec", "dev"), None),
        P(),
        P("dev", None, "sec"),
        P("dev", None, "sec"),
        P("dev", "sec", None),
        P(("sec", "dev"), None, None),
        P(("sec", "dev"), None, None),
        P(("sec", "dev")),
    )
    return jax.shard_map(
        body,
        mesh=mesh,
        in_specs=placed,
        out_specs=(P(("sec", "dev"), None), P(("sec", "dev"), None, None)),
        check_vma=False,
    )
```

```python
import functools

import jax
import jax.numpy as jnp
from jax import lax
from jax.experimental import pallas as pl
from jax.experimental.pallas import tpu as pltpu
from jax.sharding import PartitionSpec as P

MESH = pl.DeviceIdType.MESH
BF16 = jnp.bfloat16
F32 = jnp.float32
LATENT = 512
D = 7168
HID = 512
HEADS = 128
CACHE = 2048
EXPERTS = 32
TOP = 8
LANE = 128
PART = 19 * LANE
FOLD = 5 * LANE
SUBS = ((0, 12), (12, 7))
NSUB = len(SUBS)
ROUTING = NSUB
ORDERS = ("xyz", "yzx", "zxy")
SCALE = 192.0 ** (-0.5)


def span(p, s):
    off, count = SUBS[s]
    skip = LANE if (p == 2 and s == 0) else 0
    start = p * PART + off * LANE + skip - (LANE if p == 2 else 0)
    return skip, count * LANE - skip, start


def mm(a, b):
    return jnp.dot(a, b, preferred_element_type=F32)


def nt(a, b):
    return lax.dot_general(a, b, (((1,), (1,)), ((), ())), preferred_element_type=F32)


def tn(a, b):
    return lax.dot_general(a, b, (((0,), (0,)), ((), ())), preferred_element_type=F32)


def axes_of(i, p):
    a = {ORDERS[p][2]: (i >> 6) & 3, ORDERS[p][1]: (i >> 4) & 3, ORDERS[p][0]: (i >> 2) & 3}
    return a["x"], a["y"], a["z"], (i >> 8) & 1, i & 3


def token_of(i, p):
    x, y, z, c, r = axes_of(i, p)
    return y * 128 + z * 32 + x * 8 + c * 4 + r


def place_of(i, p):
    x, y, z, _, _ = axes_of(i, p)
    return y * 16 + x * 4 + z


def kernel(
    lengths_ref, capacity_ref, x_hbm, ids_hbm, gw_hbm, q_hbm, kv_hbm, gate_hbm, up_hbm, down_hbm,
    out_ref, attn_ref,
    x_ref, ids_ref, gw_ref, q, kv, gate, up, down, scores, probs, masks,
    fold, s1, xb, sel, sel2, kept_col, packed, acc_g, acc_u, hs, ht,
    cs, cr, tb, rv, us, rw, vq, d3, r3,
    lsem, s1_sem, g2_sem, g3_sem, cx_sem, r0_sem, r1_sem, r2_sem, r3_sem,
):
    y = lax.axis_index("sec")
    dev = lax.axis_index("dev")
    z, x, c = dev // 8, (dev // 2) % 4, dev % 2
    at = {"x": x, "y": y, "z": z}

    def peer(axis, step):
        to = dict(at)
        to[axis] = (at[axis] + step + 4) % 4
        return (to["y"], to["z"] * 8 + to["x"] * 2 + c)

    sibling = (y, z * 8 + x * 2 + (1 - c))
    barrier = pltpu.get_barrier_semaphore()
    for axis in "xyz":
        for step in (1, 2, 3):
            pl.semaphore_signal(barrier, inc=1, device_id=peer(axis, step), device_id_type=MESH)
    pl.semaphore_signal(barrier, inc=1, device_id=sibling, device_id_type=MESH)

    small = []
    for n, (src, dst) in enumerate(((x_hbm, x_ref), (ids_hbm, ids_ref), (gw_hbm, gw_ref))):
        small.append(pltpu.make_async_copy(src, dst, lsem.at[5 + n]))
        small[n].start()
    local = {}
    for n, (src, dst) in enumerate(
        ((q_hbm.at[0], q), (kv_hbm.at[0], kv), (gate_hbm.at[0], gate), (up_hbm.at[0], up), (down_hbm.at[0], down))
    ):
        local[n] = pltpu.make_async_copy(src, dst, lsem.at[n])
        local[n].start()

    sent = {}

    def send(key, sems, index, src, dst, to):
        copy = pltpu.make_async_remote_copy(
            src_ref=src, dst_ref=dst,
            send_sem=sems.at[(0,) + index], recv_sem=sems.at[(1,) + index],
            device_id=to, device_id_type=MESH,
        )
        copy.start()
        sent[key] = copy

    def got(key):
        sent[key].wait_recv()

    for copy in small:
        copy.wait()
    def drain(*kinds):
        for key, copy in sent.items():
            if key[0] in kinds:
                copy.wait_send()

    lane = lax.broadcasted_iota(jnp.int32, (4, LANE), 1)
    info = jnp.zeros((4, LANE), F32)
    ids = ids_ref[...]
    gw = gw_ref[...]
    high = gw.astype(BF16).astype(F32)
    mid = (gw - high).astype(BF16).astype(F32)
    low = gw - high - mid
    for k in range(TOP):
        for n, piece in enumerate((high, mid, low)):
            info = info + jnp.where(lane == ids[:, k:k + 1] + n * EXPERTS, piece[:, k:k + 1], 0.0)
    fold[...] = jnp.zeros_like(fold)
    for p in range(3):
        for f in range(4):
            first, width = f * FOLD, min(FOLD, PART - f * FOLD)
            lead = LANE if (p == 2 and f == 0) else 0
            start = p * PART + first + lead - (LANE if p == 2 else 0)
            fold[p, 4 * f:4 * f + 4, lead:width] = x_ref[:, start:start + width - lead].astype(F32)
    fold[2, 0:4, 0:LANE] = info
    for p in range(3):
        s1[p, at[ORDERS[p][0]]] = fold[p].astype(BF16)
    pl.semaphore_wait(barrier, 10)
    for step in (1, 2, 3):
        for p in range(3):
            axis = ORDERS[p][0]
            mine = s1.at[p, at[axis]]
            send(("s1", p, step), s1_sem, (p, step - 1), mine, mine, peer(axis, step))

    def attend_scores():
        local[0].wait()
        local[1].wait()
        position = lax.broadcasted_iota(jnp.int32, (1, 512), 1)
        length = lengths_ref[0]
        for n in range(CACHE // 512):
            cols = kv[:, n * 512:(n + 1) * 512]
            score = tn(q[:LATENT, :], cols[:LATENT, :]) + tn(q[LATENT:, :], cols[LATENT:, :])
            scores[:, n * 512:(n + 1) * 512] = jnp.where(position + n * 512 < length, score * SCALE, -jnp.inf)

    def attend_probs():
        score = scores[...]
        expo = jnp.exp(score - jnp.max(score, axis=1, keepdims=True))
        probs[...] = (expo / jnp.sum(expo, axis=1, keepdims=True)).astype(BF16)

    def attend_values():
        attn_ref[0] = nt(probs[...], kv[:LATENT, :]).astype(BF16)

    i0 = lax.broadcasted_iota(jnp.int32, (64, 64), 0)
    i1 = lax.broadcasted_iota(jnp.int32, (64, 64), 1)
    turn = jnp.where(((i0 >> 4) == ((i1 >> 2) & 3)) & (((i0 >> 2) & 3) == (i1 >> 4)) & ((i0 & 3) == (i1 & 3)), 1.0, 0.0).astype(BF16)

    def block(p, n, size):
        return pl.ds(pl.multiple_of(n * size, size), size)

    def piece(p, s):
        return xb[s].at[0 if s == ROUTING else p]

    def g2a(p):
        a1, a2, a3 = ORDERS[p]
        for step in (1, 2, 3):
            got(("s1", p, step))
        rows = mm(turn, s1[p].reshape(64, FOLD)).astype(BF16)
        own = block(p, at[a3] * 4 + at[a2], 16)
        for f in range(4):
            for t in range(5):
                tile = 5 * f + t
                for s, (off, count) in enumerate(SUBS):
                    if off <= tile < off + count:
                        xb[s][p, c, own, (tile - off) * LANE:(tile - off + 1) * LANE] = rows[16 * f:16 * f + 16, t * LANE:(t + 1) * LANE]
        if p == 2:
            xb[ROUTING][0, c, own, :] = rows[0:16, 0:LANE]
        for s in (ROUTING, *range(NSUB)) if p == 2 else range(NSUB):
            ref = piece(p, s).at[c, own]
            send(("g2", p, s, 0), g2_sem, (p, s, 0), ref, ref, peer(a2, 1))
            send(("g2", p, s, 1), g2_sem, (p, s, 1), ref, ref, peer(a2, -1))

    def g2b(p, s):
        _, a2, a3 = ORDERS[p]
        way = 0 if (p + s) % 2 == 0 else 1
        got(("g2", p, s, way))
        off = -1 if way == 0 else 1
        ref = piece(p, s).at[c, block(p, at[a3] * 4 + (at[a2] + off + 4) % 4, 16)]
        send(("g2", p, s, 2), g2_sem, (p, s, 2), ref, ref, peer(a2, -off))

    def g3a(p, s):
        _, a2, a3 = ORDERS[p]
        way = 0 if (p + s) % 2 == 0 else 1
        got(("g2", p, s, 1 - way))
        got(("g2", p, s, 2))
        ref = piece(p, s).at[c, block(p, at[a3], 64)]
        send(("g3", p, s, 0), g3_sem, (p, s, 0), ref, ref, peer(a3, 1))
        send(("g3", p, s, 1), g3_sem, (p, s, 1), ref, ref, peer(a3, -1))
        send(("cx", p, s, 0), cx_sem, (p, s, 0), ref, ref, sibling)

    def g3b(p, s):
        a3 = ORDERS[p][2]
        for way, off in ((0, -1), (1, 1)):
            got(("g3", p, s, way))
            whole = (at[a3] + off + 4) % 4
            ref = piece(p, s).at[c, block(p, whole * 2 + way, 32)]
            send(("g3", p, s, 2 + way), g3_sem, (p, s, 2 + way), ref, ref, peer(a3, -off))
            ref = piece(p, s).at[c, block(p, whole, 64)]
            send(("cx", p, s, 1 + way), cx_sem, (p, s, 1 + way), ref, ref, sibling)

    def g3c(p, s):
        a3 = ORDERS[p][2]
        got(("g3", p, s, 2))
        got(("g3", p, s, 3))
        ref = piece(p, s).at[c, block(p, (at[a3] + 2) % 4, 64)]
        send(("cx", p, s, 3), cx_sem, (p, s, 3), ref, ref, sibling)

    def cxw(p, s):
        for n in range(4):
            got(("cx", p, s, n))

    ones = lambda cond: jnp.where(cond, 1.0, 0.0).astype(BF16)

    def orders():
        rows = lax.broadcasted_iota(jnp.int32, (512, 1), 0)
        cols = lax.broadcasted_iota(jnp.int32, (1, 512), 1)
        masks[0] = ones(token_of(rows, 2) == token_of(cols, 0))
        masks[1] = ones(token_of(rows, 2) == token_of(cols, 1))
        masks[2] = ones(token_of(rows, 2) < token_of(cols, 2))
        masks[3] = ones(((rows >> 2) == (cols >> 2)) & (rows < cols))

    def routing():
        pick = lax.broadcasted_iota(jnp.int32, (8, LANE), 1)
        which = lax.broadcasted_iota(jnp.int32, (8, LANE), 0)
        expert = jnp.where(which == 0, dev, dev + 1 - 2 * c)
        pick = jnp.where((pick < 3 * EXPERTS) & ((pick & (EXPERTS - 1)) == expert), 1.0, 0.0).astype(BF16)
        weight = jnp.concatenate([nt(pick, xb[ROUTING][0, cc]) for cc in range(2)], axis=1)
        named = weight > 0.0
        flag = jnp.where(named, 1.0, 0.0).astype(BF16)
        arrival = mm(flag, masks[2])
        rank = mm(flag, masks[3])
        limit = capacity_ref[dev].astype(F32)
        kept = jnp.where(arrival < limit, weight, 0.0)
        code = jnp.where(named, rank + 1.0, 0.0)
        for p in range(3):
            turned = code if p == 2 else mm(code.astype(BF16), masks[p])
            for cc in range(2):
                slot = lax.broadcasted_iota(jnp.int32, (128, 1), 0)
                row = lax.broadcasted_iota(jnp.int32, (1, 256), 1)
                wanted = ((slot & 1) + 1).astype(F32)
                chosen = ((slot >> 1) == place_of(row, p)) & (turned[0:1, cc * 256:(cc + 1) * 256] == wanted)
                sel[p, cc] = ones(chosen)
                other = (slot >> 1 == place_of(row, p)) & (turned[1:2, cc * 256:(cc + 1) * 256] == wanted)
                sel2[p, cc] = ones(other)
                if p == 2:
                    kept_col[cc * 128:(cc + 1) * 128, :] = jnp.sum(
                        jnp.where(chosen, kept[0:1, cc * 256:(cc + 1) * 256], 0.0), axis=1, keepdims=True)

    def ffn(p, s):
        skip, width, start = span(p, s)
        for cc in range(2):
            packed[cc * 128:(cc + 1) * 128, :width] = mm(sel[p, cc], xb[s][p, cc, :, skip:skip + width]).astype(BF16)
        rows = packed[:, :width]
        acc_g[...] += mm(rows, gate[start:start + width, :])
        acc_u[...] += mm(rows, up[start:start + width, :])

    def act():
        g = acc_g[...]
        hidden = (g * (1.0 / (1.0 + jnp.exp(-g))) * acc_u[...] * kept_col[...]).astype(BF16)
        hs[...] = hidden.reshape(2, 128, HID)

    def spread():
        for p in range(3):
            ht[p] = tn(sel[p, c], hs[c]).astype(BF16)

    def c0(p, s):
        _, width, start = span(p, s)
        cs[s][p, :, :width] = mm(hs[1 - c], down[:, start:start + width]).astype(BF16)
        send(("r0", p, s), r0_sem, (p, s), cs[s].at[p, :, :width], cr[s].at[p, :, :width], sibling)

    def plus(ref, rows, width, *others):
        total = ref[rows, :width].astype(F32)
        for other in others:
            total = total + other[:, :width].astype(F32)
        return total.astype(BF16)

    def a1(p, s):
        _, width, start = span(p, s)
        mine = mm(ht[p], down[:, start:start + width])
        got(("r0", p, s))
        tb[s][p, :, :width] = (mine + tn(sel2[p, c], cr[s][p, :, :width])).astype(BF16)
        axis = ORDERS[p][2]
        k = at[axis]
        for n, (off, half, way) in enumerate(((2, 0, 1), (2, 1, -1), (1, 1, 1), (-1, 0, -1))):
            rows = block(p, ((k + off + 4) % 4) * 2 + half, 32)
            send(("r1", p, s, n), r1_sem, (p, s, n), tb[s].at[p, rows, :width], rv[s].at[p, n, :, :width], peer(axis, way))

    def a2(p, s):
        _, width, _ = span(p, s)
        axis = ORDERS[p][2]
        k = at[axis]
        for n, (off, half, way) in enumerate(((1, 0, 1), (-1, 1, -1))):
            got(("r1", p, s, n))
            rows = block(p, ((k + off + 4) % 4) * 2 + half, 32)
            t = tb[s].at[p]
            t[rows, :width] = plus(t, rows, width, rv[s].at[p, n])
            send(("r1", p, s, 4 + n), r1_sem, (p, s, 4 + n), tb[s].at[p, rows, :width], rv[s].at[p, 4 + n, :, :width], peer(axis, way))

    def b1(p, s):
        _, width, _ = span(p, s)
        k = at[ORDERS[p][2]]
        for n in (2, 3, 4, 5):
            got(("r1", p, s, n))
        t, u, v = tb[s].at[p], us[s].at[p], rv[s].at[p]
        u[0:32, :width] = plus(t, block(p, k * 2, 32), width, v.at[3], v.at[4])
        u[32:64, :width] = plus(t, block(p, k * 2 + 1, 32), width, v.at[2], v.at[5])
        axis = ORDERS[p][1]
        k = at[axis]
        way = 1 if (p + s) % 2 == 0 else -1
        for n, (off, to) in enumerate(((2, way), (-way, -way))):
            rows = block(p, (k + off + 4) % 4, 16)
            send(("r2", p, s, n), r2_sem, (p, s, n), u.at[rows, :width], rw[s].at[p, n, :, :width], peer(axis, to))

    def b2(p, s):
        _, width, _ = span(p, s)
        axis = ORDERS[p][1]
        k = at[axis]
        way = 1 if (p + s) % 2 == 0 else -1
        got(("r2", p, s, 0))
        rows = block(p, (k + way + 4) % 4, 16)
        u = us[s].at[p]
        u[rows, :width] = plus(u, rows, width, rw[s].at[p, 0])
        send(("r2", p, s, 2), r2_sem, (p, s, 2), u.at[rows, :width], rw[s].at[p, 2, :, :width], peer(axis, way))

    def b3(p, s):
        skip, width, _ = span(p, s)
        k = at[ORDERS[p][1]]
        got(("r2", p, s, 1))
        got(("r2", p, s, 2))
        total = plus(us[s].at[p], block(p, k, 16), width, rw[s].at[p, 1], rw[s].at[p, 2])
        off = SUBS[s][0]
        for t in range(width // LANE):
            tile = off + skip // LANE + t
            f, j = tile // 5, tile % 5
            vq[p, 16 * f:16 * f + 16, j * LANE:(j + 1) * LANE] = total[:, t * LANE:(t + 1) * LANE]

    def r3a(p):
        axis = ORDERS[p][0]
        d3[p] = mm(turn, vq[p]).astype(BF16)
        for step in (1, 2, 3):
            rows = block(p, (at[axis] + step) % 4, 16)
            send(("r3", p, step), r3_sem, (p, step - 1), d3.at[p, rows], r3.at[p, step - 1], peer(axis, step))

    def r3b(p):
        axis = ORDERS[p][0]
        total = d3[p, block(p, at[axis], 16), :].astype(F32)
        for step in (1, 2, 3):
            got(("r3", p, step))
            total = total + r3[p, step - 1].astype(F32)
        fold[p] = total
        for f in range(4):
            first, width = f * FOLD, min(FOLD, PART - f * FOLD)
            lead = LANE if (p == 2 and f == 0) else 0
            start = p * PART + first + lead - (LANE if p == 2 else 0)
            out_ref[:, start:start + width - lead] = fold[p, 4 * f:4 * f + 4, lead:width].astype(BF16)

    every = lambda step, *rest: [step(p, *rest) for p in range(3)]
    acc_g[...] = jnp.zeros_like(acc_g)
    acc_u[...] = jnp.zeros_like(acc_u)
    vq[...] = jnp.zeros_like(vq)
    for p in (2, 0, 1):
        g2a(p)
    g2b(2, ROUTING)
    every(g2b, 0)
    every(g2b, 1)
    g3a(2, ROUTING)
    every(g3a, 0)
    every(g3a, 1)
    attend_scores()
    g3b(2, ROUTING)
    attend_probs()
    g3c(2, ROUTING)
    orders()
    every(g3b, 0)
    cxw(2, ROUTING)
    routing()
    every(g3b, 1)
    attend_values()
    every(g3c, 0)
    every(g3c, 1)
    every(cxw, 0)
    local[2].wait()
    local[3].wait()
    every(ffn, 0)
    every(cxw, 1)
    every(ffn, 1)
    act()
    local[4].wait()
    every(c0, 1)
    every(c0, 0)
    spread()
    every(a1, 1)
    every(a1, 0)
    drain("s1", "g2", "g3", "cx")
    for stage in (a2, b1, b2, b3):
        every(stage, 1)
        every(stage, 0)
    every(r3a)
    drain("r0", "r1", "r2")
    every(r3b)
    drain("r3")


def body(moe_input, expert_ids, gate_weights, capacity, gate_proj, up_proj, down_proj, queries, latent_cache, lengths):
    vmem = pl.BlockSpec(memory_space=pltpu.VMEM)
    smem = pl.BlockSpec(memory_space=pltpu.SMEM)
    hbm = pl.BlockSpec(memory_space=pl.ANY)
    widths = [count * LANE for _, count in SUBS]
    per_sub = lambda *lead: [pltpu.VMEM(lead + (w,), BF16) for w in widths]
    dma = lambda *shape: pltpu.SemaphoreType.DMA((2,) + shape)
    scratch = [
        pltpu.VMEM((4, D), BF16), pltpu.VMEM((4, TOP), jnp.int32), pltpu.VMEM((4, TOP), F32),
        pltpu.VMEM((576, HEADS), BF16), pltpu.VMEM((576, CACHE), BF16),
        pltpu.VMEM((D, HID), BF16), pltpu.VMEM((D, HID), BF16), pltpu.VMEM((HID, D), BF16),
        pltpu.VMEM((HEADS, CACHE), F32), pltpu.VMEM((HEADS, CACHE), BF16), pltpu.VMEM((4, 512, 512), BF16),
        pltpu.VMEM((3, 16, FOLD), F32), pltpu.VMEM((3, 4, 16, FOLD), BF16),
        per_sub(3, 2, 256) + [pltpu.VMEM((1, 2, 256, LANE), BF16)],
        pltpu.VMEM((3, 2, 128, 256), BF16), pltpu.VMEM((3, 2, 128, 256), BF16), pltpu.VMEM((256, 1), F32), pltpu.VMEM((256, max(widths)), BF16),
        pltpu.VMEM((256, HID), F32), pltpu.VMEM((256, HID), F32), pltpu.VMEM((2, 128, HID), BF16), pltpu.VMEM((3, 256, HID), BF16),
        per_sub(3, 128), per_sub(3, 128), per_sub(3, 256), per_sub(3, 6, 32), per_sub(3, 64), per_sub(3, 3, 16),
        pltpu.VMEM((3, 64, FOLD), BF16), pltpu.VMEM((3, 64, FOLD), BF16), pltpu.VMEM((3, 3, 16, FOLD), BF16),
        pltpu.SemaphoreType.DMA((8,)),
        dma(3, 3), dma(3, NSUB + 1, 3), dma(3, NSUB + 1, 4), dma(3, NSUB + 1, 4),
        dma(3, NSUB), dma(3, NSUB, 6), dma(3, NSUB, 3), dma(3, 3),
    ]
    return pl.pallas_call(
        kernel,
        out_shape=(jax.ShapeDtypeStruct((4, D), BF16), jax.ShapeDtypeStruct((1, HEADS, LATENT), BF16)),
        in_specs=[smem, smem, hbm, hbm, hbm, hbm, hbm, hbm, hbm, hbm],
        out_specs=(vmem, vmem),
        scratch_shapes=scratch,
        compiler_params=pltpu.CompilerParams(collective_id=0, has_side_effects=True, vmem_limit_bytes=63 << 20),
        name="fused",
    )(lengths, capacity, moe_input, expert_ids, gate_weights, jnp.swapaxes(queries, 1, 2), jnp.swapaxes(latent_cache, 1, 2), gate_proj, up_proj, down_proj)


def solution(mesh):
    placed = (
        P(("sec", "dev"), None),
        P(("sec", "dev"), None),
        P(("sec", "dev"), None),
        P(),
        P("dev", None, "sec"),
        P("dev", None, "sec"),
        P("dev", "sec", None),
        P(("sec", "dev"), None, None),
        P(("sec", "dev"), None, None),
        P(("sec", "dev")),
    )
    return jax.shard_map(
        body,
        mesh=mesh,
        in_specs=placed,
        out_specs=(P(("sec", "dev"), None), P(("sec", "dev"), None, None)),
        check_vma=False,
    )
```

```python
import functools

import jax
import jax.numpy as jnp
from jax import lax
from jax.experimental import pallas as pl
from jax.experimental.pallas import tpu as pltpu
from jax.sharding import PartitionSpec as P

MESH = pl.DeviceIdType.MESH
BF16 = jnp.bfloat16
F32 = jnp.float32
LATENT = 512
D = 7168
HID = 512
HEADS = 128
CACHE = 2048
EXPERTS = 32
TOP = 8
LANE = 128
PART = 19 * LANE
FOLD = 5 * LANE
SUBS = ((0, 12), (12, 7))
NSUB = len(SUBS)
ORDERS = ("xyz", "yzx", "zxy")
SCALE = 192.0 ** (-0.5)


def span(p, s):
    off, count = SUBS[s]
    skip = LANE if (p == 2 and s == 0) else 0
    start = p * PART + off * LANE + skip - (LANE if p == 2 else 0)
    return skip, count * LANE - skip, start


def mm(a, b):
    return jnp.dot(a, b, preferred_element_type=F32)


def nt(a, b):
    return lax.dot_general(a, b, (((1,), (1,)), ((), ())), preferred_element_type=F32)


def tn(a, b):
    return lax.dot_general(a, b, (((0,), (0,)), ((), ())), preferred_element_type=F32)


def axes_of(i, p):
    a = {ORDERS[p][2]: (i >> 6) & 3, ORDERS[p][1]: (i >> 4) & 3, ORDERS[p][0]: (i >> 2) & 3}
    return a["x"], a["y"], a["z"], (i >> 8) & 1, i & 3


def token_of(i, p):
    x, y, z, c, r = axes_of(i, p)
    return y * 128 + z * 32 + x * 8 + c * 4 + r


def place_of(i, p):
    x, y, z, _, _ = axes_of(i, p)
    return y * 16 + x * 4 + z


def kernel(
    lengths_ref, capacity_ref, x_hbm, ids_hbm, gw_hbm, q_hbm, kv_hbm, gate_hbm, up_hbm, down_hbm,
    out_ref, attn_ref,
    x_ref, ids_ref, gw_ref, q, kv, gate, up, down, scores, probs, masks,
    fold, s1, xb, sel, sel2, kept_col, packed, acc_g, acc_u, hs, ht,
    cs, cr, tb, rv, us, rw, vq, d3, r3,
    lsem, s1_sem, g2_sem, g3_sem, cx_sem, r0_sem, r1_sem, r2_sem, r3_sem,
):
    y = lax.axis_index("sec")
    dev = lax.axis_index("dev")
    z, x, c = dev // 8, (dev // 2) % 4, dev % 2
    at = {"x": x, "y": y, "z": z}

    def peer(axis, step):
        to = dict(at)
        to[axis] = (at[axis] + step + 4) % 4
        return (to["y"], to["z"] * 8 + to["x"] * 2 + c)

    sibling = (y, z * 8 + x * 2 + (1 - c))
    barrier = pltpu.get_barrier_semaphore()
    for axis in "xyz":
        for step in (1, 2, 3):
            pl.semaphore_signal(barrier, inc=1, device_id=peer(axis, step), device_id_type=MESH)
    pl.semaphore_signal(barrier, inc=1, device_id=sibling, device_id_type=MESH)

    small = []
    for n, (src, dst) in enumerate(((x_hbm, x_ref), (ids_hbm, ids_ref), (gw_hbm, gw_ref))):
        small.append(pltpu.make_async_copy(src, dst, lsem.at[5 + n]))
        small[n].start()
    local = {}
    for n, (src, dst) in enumerate(
        ((q_hbm.at[0], q), (kv_hbm.at[0], kv), (gate_hbm.at[0], gate), (up_hbm.at[0], up), (down_hbm.at[0], down))
    ):
        local[n] = pltpu.make_async_copy(src, dst, lsem.at[n])
        local[n].start()

    sent = {}

    def send(key, sems, index, src, dst, to):
        copy = pltpu.make_async_remote_copy(
            src_ref=src, dst_ref=dst,
            send_sem=sems.at[(0,) + index], recv_sem=sems.at[(1,) + index],
            device_id=to, device_id_type=MESH,
        )
        copy.start()
        sent[key] = copy

    def got(key):
        sent[key].wait_recv()

    for copy in small:
        copy.wait()
    def drain(*kinds):
        for key, copy in sent.items():
            if key[0] in kinds:
                copy.wait_send()

    lane = lax.broadcasted_iota(jnp.int32, (4, LANE), 1)
    info = jnp.zeros((4, LANE), F32)
    ids = ids_ref[...]
    gw = gw_ref[...]
    high = gw.astype(BF16).astype(F32)
    mid = (gw - high).astype(BF16).astype(F32)
    low = gw - high - mid
    for k in range(TOP):
        for n, piece in enumerate((high, mid, low)):
            info = info + jnp.where(lane == ids[:, k:k + 1] + n * EXPERTS, piece[:, k:k + 1], 0.0)
    fold[...] = jnp.zeros_like(fold)
    for p in range(3):
        for f in range(4):
            first, width = f * FOLD, min(FOLD, PART - f * FOLD)
            lead = LANE if (p == 2 and f == 0) else 0
            start = p * PART + first + lead - (LANE if p == 2 else 0)
            fold[p, 4 * f:4 * f + 4, lead:width] = x_ref[:, start:start + width - lead].astype(F32)
    fold[2, 0:4, 0:LANE] = info
    for p in range(3):
        s1[p, at[ORDERS[p][0]]] = fold[p].astype(BF16)
    pl.semaphore_wait(barrier, 10)
    for step in (1, 2, 3):
        for p in range(3):
            axis = ORDERS[p][0]
            mine = s1.at[p, at[axis]]
            send(("s1", p, step), s1_sem, (p, step - 1), mine, mine, peer(axis, step))

    def attend_scores():
        local[0].wait()
        local[1].wait()
        position = lax.broadcasted_iota(jnp.int32, (1, 512), 1)
        length = lengths_ref[0]
        for n in range(CACHE // 512):
            cols = kv[:, n * 512:(n + 1) * 512]
            score = tn(q[:LATENT, :], cols[:LATENT, :]) + tn(q[LATENT:, :], cols[LATENT:, :])
            scores[:, n * 512:(n + 1) * 512] = jnp.where(position + n * 512 < length, score * SCALE, -jnp.inf)

    def attend_probs():
        score = scores[...]
        expo = jnp.exp(score - jnp.max(score, axis=1, keepdims=True))
        probs[...] = (expo / jnp.sum(expo, axis=1, keepdims=True)).astype(BF16)

    def attend_values():
        attn_ref[0] = nt(probs[...], kv[:LATENT, :]).astype(BF16)

    i0 = lax.broadcasted_iota(jnp.int32, (64, 64), 0)
    i1 = lax.broadcasted_iota(jnp.int32, (64, 64), 1)
    turn = jnp.where(((i0 >> 4) == ((i1 >> 2) & 3)) & (((i0 >> 2) & 3) == (i1 >> 4)) & ((i0 & 3) == (i1 & 3)), 1.0, 0.0).astype(BF16)

    def block(p, n, size):
        return pl.ds(pl.multiple_of(n * size, size), size)

    def g2a(p):
        a1, a2, a3 = ORDERS[p]
        for step in (1, 2, 3):
            got(("s1", p, step))
        rows = mm(turn, s1[p].reshape(64, FOLD)).astype(BF16)
        own = block(p, at[a3] * 4 + at[a2], 16)
        for f in range(4):
            for t in range(5):
                tile = 5 * f + t
                for s, (off, count) in enumerate(SUBS):
                    if off <= tile < off + count:
                        xb[s][p, c, own, (tile - off) * LANE:(tile - off + 1) * LANE] = rows[16 * f:16 * f + 16, t * LANE:(t + 1) * LANE]
        for s in range(NSUB):
            ref = xb[s].at[p, c, own]
            send(("g2", p, s, 0), g2_sem, (p, s, 0), ref, ref, peer(a2, 1))
            send(("g2", p, s, 1), g2_sem, (p, s, 1), ref, ref, peer(a2, -1))

    def g2b(p, s):
        _, a2, a3 = ORDERS[p]
        way = 0 if (p + s) % 2 == 0 else 1
        got(("g2", p, s, way))
        off = -1 if way == 0 else 1
        ref = xb[s].at[p, c, block(p, at[a3] * 4 + (at[a2] + off + 4) % 4, 16)]
        send(("g2", p, s, 2), g2_sem, (p, s, 2), ref, ref, peer(a2, -off))

    def g3a(p, s):
        _, a2, a3 = ORDERS[p]
        way = 0 if (p + s) % 2 == 0 else 1
        got(("g2", p, s, 1 - way))
        got(("g2", p, s, 2))
        ref = xb[s].at[p, c, block(p, at[a3], 64)]
        send(("g3", p, s, 0), g3_sem, (p, s, 0), ref, ref, peer(a3, 1))
        send(("g3", p, s, 1), g3_sem, (p, s, 1), ref, ref, peer(a3, -1))
        send(("cx", p, s, 0), cx_sem, (p, s, 0), ref, ref, sibling)

    def g3b(p, s):
        a3 = ORDERS[p][2]
        for way, off in ((0, -1), (1, 1)):
            got(("g3", p, s, way))
            whole = (at[a3] + off + 4) % 4
            ref = xb[s].at[p, c, block(p, whole * 2 + way, 32)]
            send(("g3", p, s, 2 + way), g3_sem, (p, s, 2 + way), ref, ref, peer(a3, -off))
            ref = xb[s].at[p, c, block(p, whole, 64)]
            send(("cx", p, s, 1 + way), cx_sem, (p, s, 1 + way), ref, ref, sibling)

    def g3c(p, s):
        a3 = ORDERS[p][2]
        got(("g3", p, s, 2))
        got(("g3", p, s, 3))
        ref = xb[s].at[p, c, block(p, (at[a3] + 2) % 4, 64)]
        send(("cx", p, s, 3), cx_sem, (p, s, 3), ref, ref, sibling)

    def cxw(p, s):
        for n in range(4):
            got(("cx", p, s, n))

    ones = lambda cond: jnp.where(cond, 1.0, 0.0).astype(BF16)

    def orders():
        rows = lax.broadcasted_iota(jnp.int32, (512, 1), 0)
        cols = lax.broadcasted_iota(jnp.int32, (1, 512), 1)
        masks[0] = ones(token_of(rows, 2) == token_of(cols, 0))
        masks[1] = ones(token_of(rows, 2) == token_of(cols, 1))
        masks[2] = ones(token_of(rows, 2) < token_of(cols, 2))
        masks[3] = ones(((rows >> 2) == (cols >> 2)) & (rows < cols))

    def routing():
        pick = lax.broadcasted_iota(jnp.int32, (8, LANE), 1)
        which = lax.broadcasted_iota(jnp.int32, (8, LANE), 0)
        expert = jnp.where(which == 0, dev, dev + 1 - 2 * c)
        pick = jnp.where((pick < 3 * EXPERTS) & ((pick & (EXPERTS - 1)) == expert), 1.0, 0.0).astype(BF16)
        weight = jnp.concatenate([nt(pick, xb[0][2, cc, :, 0:LANE]) for cc in range(2)], axis=1)
        named = weight > 0.0
        flag = jnp.where(named, 1.0, 0.0).astype(BF16)
        arrival = mm(flag, masks[2])
        rank = mm(flag, masks[3])
        limit = capacity_ref[dev].astype(F32)
        kept = jnp.where(arrival < limit, weight, 0.0)
        code = jnp.where(named, rank + 1.0, 0.0)
        for p in range(3):
            turned = code if p == 2 else mm(code.astype(BF16), masks[p])
            for cc in range(2):
                slot = lax.broadcasted_iota(jnp.int32, (128, 1), 0)
                row = lax.broadcasted_iota(jnp.int32, (1, 256), 1)
                wanted = ((slot & 1) + 1).astype(F32)
                chosen = ((slot >> 1) == place_of(row, p)) & (turned[0:1, cc * 256:(cc + 1) * 256] == wanted)
                sel[p, cc] = ones(chosen)
                other = (slot >> 1 == place_of(row, p)) & (turned[1:2, cc * 256:(cc + 1) * 256] == wanted)
                sel2[p, cc] = ones(other)
                if p == 2:
                    kept_col[cc * 128:(cc + 1) * 128, :] = jnp.sum(
                        jnp.where(chosen, kept[0:1, cc * 256:(cc + 1) * 256], 0.0), axis=1, keepdims=True)

    def ffn(p, s):
        skip, width, start = span(p, s)
        for cc in range(2):
            packed[cc * 128:(cc + 1) * 128, :width] = mm(sel[p, cc], xb[s][p, cc, :, skip:skip + width]).astype(BF16)
        rows = packed[:, :width]
        acc_g[...] += mm(rows, gate[start:start + width, :])
        acc_u[...] += mm(rows, up[start:start + width, :])

    def act():
        g = acc_g[...]
        hidden = (g * (1.0 / (1.0 + jnp.exp(-g))) * acc_u[...] * kept_col[...]).astype(BF16)
        hs[...] = hidden.reshape(2, 128, HID)

    def spread():
        for p in range(3):
            ht[p] = tn(sel[p, c], hs[c]).astype(BF16)

    def c0(p, s):
        _, width, start = span(p, s)
        cs[s][p, :, :width] = mm(hs[1 - c], down[:, start:start + width]).astype(BF16)
        send(("r0", p, s), r0_sem, (p, s), cs[s].at[p, :, :width], cr[s].at[p, :, :width], sibling)

    def plus(ref, rows, width, *others):
        total = ref[rows, :width].astype(F32)
        for other in others:
            total = total + other[:, :width].astype(F32)
        return total.astype(BF16)

    def a1(p, s):
        _, width, start = span(p, s)
        mine = mm(ht[p], down[:, start:start + width])
        got(("r0", p, s))
        tb[s][p, :, :width] = (mine + tn(sel2[p, c], cr[s][p, :, :width])).astype(BF16)
        axis = ORDERS[p][2]
        k = at[axis]
        for n, (off, half, way) in enumerate(((2, 0, 1), (2, 1, -1), (1, 1, 1), (-1, 0, -1))):
            rows = block(p, ((k + off + 4) % 4) * 2 + half, 32)
            send(("r1", p, s, n), r1_sem, (p, s, n), tb[s].at[p, rows, :width], rv[s].at[p, n, :, :width], peer(axis, way))

    def a2(p, s):
        _, width, _ = span(p, s)
        axis = ORDERS[p][2]
        k = at[axis]
        for n, (off, half, way) in enumerate(((1, 0, 1), (-1, 1, -1))):
            got(("r1", p, s, n))
            rows = block(p, ((k + off + 4) % 4) * 2 + half, 32)
            t = tb[s].at[p]
            t[rows, :width] = plus(t, rows, width, rv[s].at[p, n])
            send(("r1", p, s, 4 + n), r1_sem, (p, s, 4 + n), tb[s].at[p, rows, :width], rv[s].at[p, 4 + n, :, :width], peer(axis, way))

    def b1(p, s):
        _, width, _ = span(p, s)
        k = at[ORDERS[p][2]]
        for n in (2, 3, 4, 5):
            got(("r1", p, s, n))
        t, u, v = tb[s].at[p], us[s].at[p], rv[s].at[p]
        u[0:32, :width] = plus(t, block(p, k * 2, 32), width, v.at[3], v.at[4])
        u[32:64, :width] = plus(t, block(p, k * 2 + 1, 32), width, v.at[2], v.at[5])
        axis = ORDERS[p][1]
        k = at[axis]
        way = 1 if (p + s) % 2 == 0 else -1
        for n, (off, to) in enumerate(((2, way), (-way, -way))):
            rows = block(p, (k + off + 4) % 4, 16)
            send(("r2", p, s, n), r2_sem, (p, s, n), u.at[rows, :width], rw[s].at[p, n, :, :width], peer(axis, to))

    def b2(p, s):
        _, width, _ = span(p, s)
        axis = ORDERS[p][1]
        k = at[axis]
        way = 1 if (p + s) % 2 == 0 else -1
        got(("r2", p, s, 0))
        rows = block(p, (k + way + 4) % 4, 16)
        u = us[s].at[p]
        u[rows, :width] = plus(u, rows, width, rw[s].at[p, 0])
        send(("r2", p, s, 2), r2_sem, (p, s, 2), u.at[rows, :width], rw[s].at[p, 2, :, :width], peer(axis, way))

    def b3(p, s):
        skip, width, _ = span(p, s)
        k = at[ORDERS[p][1]]
        got(("r2", p, s, 1))
        got(("r2", p, s, 2))
        total = plus(us[s].at[p], block(p, k, 16), width, rw[s].at[p, 1], rw[s].at[p, 2])
        off = SUBS[s][0]
        for t in range(width // LANE):
            tile = off + skip // LANE + t
            f, j = tile // 5, tile % 5
            vq[p, 16 * f:16 * f + 16, j * LANE:(j + 1) * LANE] = total[:, t * LANE:(t + 1) * LANE]

    def r3a(p):
        axis = ORDERS[p][0]
        d3[p] = mm(turn, vq[p]).astype(BF16)
        for step in (1, 2, 3):
            rows = block(p, (at[axis] + step) % 4, 16)
            send(("r3", p, step), r3_sem, (p, step - 1), d3.at[p, rows], r3.at[p, step - 1], peer(axis, step))

    def r3b(p):
        axis = ORDERS[p][0]
        total = d3[p, block(p, at[axis], 16), :].astype(F32)
        for step in (1, 2, 3):
            got(("r3", p, step))
            total = total + r3[p, step - 1].astype(F32)
        fold[p] = total
        for f in range(4):
            first, width = f * FOLD, min(FOLD, PART - f * FOLD)
            lead = LANE if (p == 2 and f == 0) else 0
            start = p * PART + first + lead - (LANE if p == 2 else 0)
            out_ref[:, start:start + width - lead] = fold[p, 4 * f:4 * f + 4, lead:width].astype(BF16)

    every = lambda step, *rest: [step(p, *rest) for p in range(3)]
    acc_g[...] = jnp.zeros_like(acc_g)
    acc_u[...] = jnp.zeros_like(acc_u)
    vq[...] = jnp.zeros_like(vq)
    attend_scores()
    every(g2a)
    for s in range(NSUB):
        every(g2b, s)
    for s in range(NSUB):
        every(g3a, s)
    orders()
    for s in range(NSUB):
        every(g3b, s)
    for s in range(NSUB):
        every(g3c, s)
    every(cxw, 0)
    routing()
    local[2].wait()
    local[3].wait()
    every(ffn, 0)
    every(cxw, 1)
    every(ffn, 1)
    act()
    local[4].wait()
    every(c0, 1)
    every(c0, 0)
    spread()
    every(a1, 1)
    every(a1, 0)
    drain("s1", "g2", "g3", "cx")
    attend_probs()
    attend_values()
    for stage in (a2, b1, b2, b3):
        every(stage, 1)
        every(stage, 0)
    every(r3a)
    drain("r0", "r1", "r2")
    every(r3b)
    drain("r3")


def body(moe_input, expert_ids, gate_weights, capacity, gate_proj, up_proj, down_proj, queries, latent_cache, lengths):
    vmem = pl.BlockSpec(memory_space=pltpu.VMEM)
    smem = pl.BlockSpec(memory_space=pltpu.SMEM)
    hbm = pl.BlockSpec(memory_space=pl.ANY)
    widths = [count * LANE for _, count in SUBS]
    per_sub = lambda *lead: [pltpu.VMEM(lead + (w,), BF16) for w in widths]
    dma = lambda *shape: pltpu.SemaphoreType.DMA((2,) + shape)
    scratch = [
        pltpu.VMEM((4, D), BF16), pltpu.VMEM((4, TOP), jnp.int32), pltpu.VMEM((4, TOP), F32),
        pltpu.VMEM((576, HEADS), BF16), pltpu.VMEM((576, CACHE), BF16),
        pltpu.VMEM((D, HID), BF16), pltpu.VMEM((D, HID), BF16), pltpu.VMEM((HID, D), BF16),
        pltpu.VMEM((HEADS, CACHE), F32), pltpu.VMEM((HEADS, CACHE), BF16), pltpu.VMEM((4, 512, 512), BF16),
        pltpu.VMEM((3, 16, FOLD), F32), pltpu.VMEM((3, 4, 16, FOLD), BF16),
        per_sub(3, 2, 256),
        pltpu.VMEM((3, 2, 128, 256), BF16), pltpu.VMEM((3, 2, 128, 256), BF16), pltpu.VMEM((256, 1), F32), pltpu.VMEM((256, max(widths)), BF16),
        pltpu.VMEM((256, HID), F32), pltpu.VMEM((256, HID), F32), pltpu.VMEM((2, 128, HID), BF16), pltpu.VMEM((3, 256, HID), BF16),
        per_sub(3, 128), per_sub(3, 128), per_sub(3, 256), per_sub(3, 6, 32), per_sub(3, 64), per_sub(3, 3, 16),
        pltpu.VMEM((3, 64, FOLD), BF16), pltpu.VMEM((3, 64, FOLD), BF16), pltpu.VMEM((3, 3, 16, FOLD), BF16),
        pltpu.SemaphoreType.DMA((8,)),
        dma(3, 3), dma(3, NSUB, 3), dma(3, NSUB, 4), dma(3, NSUB, 4),
        dma(3, NSUB), dma(3, NSUB, 6), dma(3, NSUB, 3), dma(3, 3),
    ]
    return pl.pallas_call(
        kernel,
        out_shape=(jax.ShapeDtypeStruct((4, D), BF16), jax.ShapeDtypeStruct((1, HEADS, LATENT), BF16)),
        in_specs=[smem, smem, hbm, hbm, hbm, hbm, hbm, hbm, hbm, hbm],
        out_specs=(vmem, vmem),
        scratch_shapes=scratch,
        compiler_params=pltpu.CompilerParams(collective_id=0, has_side_effects=True, vmem_limit_bytes=63 << 20),
        name="fused",
    )(lengths, capacity, moe_input, expert_ids, gate_weights, jnp.swapaxes(queries, 1, 2), jnp.swapaxes(latent_cache, 1, 2), gate_proj, up_proj, down_proj)


def solution(mesh):
    placed = (
        P(("sec", "dev"), None),
        P(("sec", "dev"), None),
        P(("sec", "dev"), None),
        P(),
        P("dev", None, "sec"),
        P("dev", None, "sec"),
        P("dev", "sec", None),
        P(("sec", "dev"), None, None),
        P(("sec", "dev"), None, None),
        P(("sec", "dev")),
    )
    return jax.shard_map(
        body,
        mesh=mesh,
        in_specs=placed,
        out_specs=(P(("sec", "dev"), None), P(("sec", "dev"), None, None)),
        check_vma=False,
    )
```
